32 devices in a mesh: fsdp: 8 (over y, x, core), dp: 4 (over z).
Axes of the slice: x: 2, y: 2, z: 4, core: 2. Of those that a mesh axis runs over, the one named last changes fastest.
Arguments:
- tokens: bfloat16 [32768, 960], P(('fsdp', 'dp')), may hold values from -6 to 6
- first_len: int32 [32], P(('fsdp', 'dp')), may hold values from 256 to 1024, as said below
- gain_attn: bfloat16 [960], P('fsdp'), may hold values from 0.099609375 to 1.8984375
- w_query: bfloat16 [960, 960], P('fsdp', 'dp'), may hold values from -0.1875 to 0.1875
- w_key: bfloat16 [960, 320], P('fsdp', 'dp'), may hold values from -0.1875 to 0.1875
- w_value: bfloat16 [960, 320], P('fsdp', 'dp'), may hold values from -0.1875 to 0.1875
- w_out: bfloat16 [960, 960], P('fsdp', 'dp'), may hold values from -1.5 to 1.5
- gain_mlp: bfloat16 [960], P('fsdp'), may hold values from 0.099609375 to 1.8984375
- w_gate: bfloat16 [960, 2560], P('fsdp', 'dp'), may hold values from -0.1875 to 0.1875
- w_up: bfloat16 [960, 2560], P('fsdp', 'dp'), may hold values from -0.1875 to 0.1875
- w_down: bfloat16 [2560, 960], P('fsdp', 'dp'), may hold values from -0.125 to 0.125
- cotangent: bfloat16 [32768, 960], P(('fsdp', 'dp')), may hold values from -6 to 6
Outputs:
- mixed: bfloat16 [32768, 960], P(('fsdp', 'dp'))
- grad_tokens: bfloat16 [32768, 960], P(('fsdp', 'dp'))
- grad_gain_attn: float32 [960], P('fsdp')
- grad_query: float32 [960, 960], P('fsdp', 'dp')
- grad_key: float32 [960, 320], P('fsdp', 'dp')
- grad_value: float32 [960, 320], P('fsdp', 'dp')
- grad_out: float32 [960, 960], P('fsdp', 'dp')
- grad_gain_mlp: float32 [960], P('fsdp')
- grad_gate: float32 [960, 2560], P('fsdp', 'dp')
- grad_up: float32 [960, 2560], P('fsdp', 'dp')
- grad_down: float32 [2560, 960], P('fsdp', 'dp')
The draws below stay inside these ranges and needn't reach their ends.
Inputs may be any that keep to these rules, and one draw needn't show every extreme that they name: `first_len`: every entry is a multiple of 128; either it equals 1024 (the group holds one sequence) or it and 1024 minus it are both at least 256; at least one group holds a single sequence.
All inputs are finite; a program needn't handle non-finite values.
Results may differ from the reference program's by a relative error of at most 0.02.
Values may be sent and summed in bfloat16 or wider, within the bound.
No kernel may reach another device: no remote copies, remote signals or barrier semaphores. Data moves between devices by JAX's collectives and lax.ppermute only.
A program may use at most 320 MiB of HBM per device.

```python
import jax
import jax.numpy as jnp
from jax import lax

D = 960
FF = 2560
HEADS = 15
KV_HEADS = 5
HEAD_DIM = 64
TOK_DEV = 1024
BLOCK = 128
MIN_LEN = 256
KV_WIDTH = 320
TOKENS = 32768
N_FSDP = 8
N_DP = 4
DEVICES = 32


def draw_first_len(key, part):
    key = jax.random.fold_in(key, 7)
    blocks = TOK_DEV // BLOCK
    least = MIN_LEN // BLOCK
    key_cut, key_whole, key_chosen = jax.random.split(key, 3)
    cutting = jax.random.randint(key_cut, (DEVICES,), least, blocks - least + 1)
    single = jax.random.randint(key_whole, (DEVICES,), 0, 2)
    chosen = jax.random.randint(key_chosen, (), 0, DEVICES)
    single = jnp.where(jnp.arange(DEVICES) == chosen, 1, single)
    return (jnp.where(single == 1, blocks, cutting) * BLOCK).astype(jnp.int32)


def levels(own_key, shape, cuts, low, largest):
    factor_of, own = 1.0, jax.random.fold_in(own_key, 6)
    for dim, parts in cuts:
        steps = jnp.exp(jax.random.uniform(jax.random.fold_in(own, dim), (parts,), jnp.float32, low / len(cuts), largest / len(cuts)))
        factor_of = factor_of * jnp.repeat(steps, shape[dim] // parts).reshape([-1 if axis == dim else 1 for axis in range(len(shape))])
    return factor_of


def normal_values(rng, dims, spread, most, pieces=(), kind=jnp.bfloat16):
    entries = spread * jax.random.normal(rng, dims, jnp.float32)
    if pieces:
        entries = entries * levels(rng, dims, pieces, -0.22, 0.18)
    return jnp.clip(entries, -most, most).astype(kind)


def setup_inputs(seed: int = 0) -> dict:
    splits = jax.random.split(jax.random.key(seed), 13)
    return {
        "tokens": normal_values(splits[0], (TOKENS, D), 1.0, 6.0, ((0, 32),)),
        "first_len": draw_first_len(jax.random.fold_in(splits[12], 71), 0),
        "gain_attn": jnp.clip(1.0 + 0.18 * jax.random.normal(splits[2], (D,), jnp.float32), 0.099609375, 1.8984375).astype(jnp.bfloat16),
        "w_query": normal_values(splits[3], (D, D), D ** -0.5, 0.1875, ((0, 8), (1, 4))),
        "w_key": normal_values(splits[4], (D, KV_WIDTH), D ** -0.5, 0.1875, ((0, 8), (1, 4))),
        "w_value": normal_values(splits[5], (D, KV_WIDTH), D ** -0.5, 0.1875, ((0, 8), (1, 4))),
        "w_out": normal_values(splits[6], (D, D), (D // 64) ** -0.5, 1.5, ((0, 8), (1, 4))),
        "gain_mlp": jnp.clip(1.0 + 0.18 * jax.random.normal(splits[7], (D,), jnp.float32), 0.099609375, 1.8984375).astype(jnp.bfloat16),
        "w_gate": normal_values(splits[8], (D, FF), D ** -0.5, 0.1875, ((0, 8), (1, 4))),
        "w_up": normal_values(splits[9], (D, FF), D ** -0.5, 0.1875, ((0, 8), (1, 4))),
        "w_down": normal_values(splits[10], (FF, D), FF ** -0.5, 0.125, ((0, 8), (1, 4))),
        "cotangent": normal_values(splits[11], (TOKENS, D), 1.0, 6.0, ((0, 32),)),
    }


@jax.custom_vjp
def low(v):
    return lax.optimization_barrier(v.astype(jnp.bfloat16)).astype(jnp.float32)

@jax.custom_vjp
def low_back(v):
    return v

def low_keep(v):
    return (low(v), None)

def low_pass(kept, grad):
    return (grad,)

def back_keep(v):
    return (v, None)

def back_low(kept, grad):
    return (low(grad),)
low.defvjp(low_keep, low_pass)
low_back.defvjp(back_keep, back_low)
epsilon = 1e-05
rope_base = 10000.0

def matmul(left, right):
    return jnp.dot(left, right, precision=lax.Precision.HIGHEST, preferred_element_type=jnp.float32)

def rms_scale(values, gain):
    inverse = lax.rsqrt(lax.optimization_barrier(jnp.mean(values * values, axis=-1, keepdims=True)) + epsilon)
    return values * inverse * gain

def rotate(values, cosine, sine):
    middle = values.shape[-1] // 2
    turned = jnp.concatenate([-values[..., middle:], values[..., :middle]], axis=-1)
    return values * cosine + turned * sine

def rope_tables(first, length):
    places = jnp.arange(length, dtype=jnp.int32)
    position = jnp.where(places < first, places, places - first).astype(jnp.float32)
    frequency = rope_base ** (-jnp.arange(0, HEAD_DIM, 2, dtype=jnp.float32) / HEAD_DIM)
    angles = position[:, None] * frequency[None, :]
    angles = jnp.concatenate([angles, angles], axis=-1)
    return (jnp.cos(angles)[:, None, :], jnp.sin(angles)[:, None, :])

def layer(inputs, first, params):
    gain_one, w_query, w_key, w_value, w_out, gain_two, w_gate, w_up, w_down = params
    length = inputs.shape[0]
    groups = HEADS // KV_HEADS
    scale = HEAD_DIM ** (-0.5)
    cosine, sine = rope_tables(first, length)
    normed = low(rms_scale(inputs, gain_one))
    queries = low_back(matmul(normed, w_query)).reshape(length, HEADS, HEAD_DIM)
    keys = low_back(matmul(normed, w_key)).reshape(length, KV_HEADS, HEAD_DIM)
    values = low(low_back(matmul(normed, w_value))).reshape(length, KV_HEADS, HEAD_DIM)
    queries = low(rotate(queries, cosine, sine)).reshape(length, KV_HEADS, groups, HEAD_DIM)
    keys = low(rotate(keys, cosine, sine))
    scores = jnp.einsum('qkgd,skd->kgqs', queries, keys, precision=lax.Precision.HIGHEST) * scale
    scores = low_back(scores)
    rows = jnp.arange(length, dtype=jnp.int32)[:, None]
    columns = jnp.arange(length, dtype=jnp.int32)[None, :]
    allowed = (columns <= rows) & ((columns >= first) | (rows < first))
    scores = jnp.where(allowed, scores, -1e+30)
    highest = lax.optimization_barrier(jnp.max(scores, axis=-1, keepdims=True))
    weights_exp = jnp.exp(scores - highest)
    probs = weights_exp / lax.optimization_barrier(jnp.sum(weights_exp, axis=-1, keepdims=True))
    attended = jnp.einsum('kgqs,skd->qkgd', low(probs), values, precision=lax.Precision.HIGHEST)
    attended = low_back(low(attended.reshape(length, D)))
    middle = inputs + low_back(matmul(attended, w_out))
    normed_two = low(rms_scale(middle, gain_two))
    gate = low_back(matmul(normed_two, w_gate))
    upward = low_back(matmul(normed_two, w_up))
    hidden = low(jax.nn.silu(gate) * upward)
    return middle + matmul(hidden, w_down)

def reference(tokens, first_len, gain_attn, w_query, w_key, w_value, w_out, gain_mlp, w_gate, w_up, w_down, cotangent):
    params = tuple((weight.astype(jnp.float32) for weight in (gain_attn, w_query, w_key, w_value, w_out, gain_mlp, w_gate, w_up, w_down)))
    groups_all = N_FSDP * N_DP
    inputs = tokens.astype(jnp.float32).reshape(groups_all, TOK_DEV, D)
    upstream = cotangent.astype(jnp.float32).reshape(groups_all, TOK_DEV, D)

    def forward(inputs, params):

        def advance(carried, element):
            return (carried, layer(element[0], element[1], params))
        return lax.scan(jax.checkpoint(advance), jnp.zeros((), jnp.float32), (inputs, first_len))[1]
    outputs, pullback = jax.vjp(forward, inputs, params)
    grad_inputs, grad_params = pullback(upstream)
    mixed = outputs.reshape(groups_all * TOK_DEV, D).astype(jnp.bfloat16)
    grad_tokens = grad_inputs.reshape(groups_all * TOK_DEV, D).astype(jnp.bfloat16)
    return (mixed, grad_tokens, grad_params[0], grad_params[1], grad_params[2], grad_params[3], grad_params[4], grad_params[5], grad_params[6], grad_params[7], grad_params[8])
```

```python
import functools

import jax
import jax.numpy as jnp
from jax import lax
from jax.experimental import pallas as pl
from jax.experimental.pallas import tpu as pltpu
from jax.sharding import PartitionSpec as P

D = 960
FF = 2560
HEADS = 15
KV_HEADS = 5
GROUP = HEADS // KV_HEADS
HEAD_DIM = 64
HALF = HEAD_DIM // 2
TILE = 256
QUAD = 4
DB = D // QUAD
FB = FF // QUAD
QB = D // QUAD
KB = KV_HEADS * HEAD_DIM // QUAD
ROWS = 128
SPARE = 16
QKV = QB + 2 * KB
QKV_ROWS = 208
LEAD = FB - 512
SKIP = DB - LEAD
NEG = -1e30
EPS = 1e-05
ROPE_BASE = 10000.0
BIG = 60 * 1024 * 1024

F32 = jnp.float32
BF16 = jnp.bfloat16


def nn(a, b):
    return jnp.dot(a, b, preferred_element_type=F32)


def nt(a, b):
    return lax.dot_general(a, b, (((1,), (1,)), ((), ())), preferred_element_type=F32)


def rope_tables(first, length):
    places = jnp.arange(length, dtype=jnp.int32)
    position = jnp.where(places < first, places, places - first).astype(F32)
    frequency = ROPE_BASE ** (-jnp.arange(0, HEAD_DIM, 2, dtype=F32) / HEAD_DIM)
    angles = frequency[:, None] * position[None, :]
    return jnp.cos(angles), jnp.sin(angles)


def params():
    return pltpu.CompilerParams(vmem_limit_bytes=BIG)


def any_spec():
    return pl.BlockSpec(memory_space=pl.ANY)


def copies(idx, mine, other, sems, target):
    plans = ([], [])
    for mine_core in range(2):
        slot = 0
        for core, pieces in ((mine_core, mine), (1 - mine_core, other)):
            for k in range(QUAD):
                for kz in range(QUAD):
                    if k < 3:
                        ref = pieces[k].at[kz]
                    elif kz < 2:
                        ref = pieces[3].at[kz]
                    else:
                        ref = pieces[4].at[kz - 2]
                    for source, dest in target(core, idx[4 + kz], idx[k], kz):
                        src = ref if source is None else ref.at[pl.ds(*source), :]
                        plans[mine_core].append(
                            pltpu.make_async_copy(src, dest, sems.at[slot])
                        )
                        slot += 1
    return plans


def rows_target(weight, gains=None):
    def target(core, z, yx, kz):
        base = pl.multiple_of(yx * DB, 16)
        if core == 0:
            return [((0, ROWS), weight.at[z, pl.ds(base, ROWS), :])]
        found = [((SPARE, DB - ROWS), weight.at[z, pl.ds(base + ROWS, DB - ROWS), :])]
        if gains is not None and kz == 0:
            found.append(((0, SPARE), gains.at[yx]))
        return found

    return target


def down_target(weight):
    def target(core, z, yx, kz):
        base = pl.multiple_of(z * DB, 16)
        if core == 0:
            return [((0, ROWS), weight.at[yx, pl.ds(base, ROWS), :])]
        return [((SPARE, DB - ROWS), weight.at[yx, pl.ds(base + ROWS, DB - ROWS), :])]

    return target


def pair_target(weight):
    def target(core, z, yx, kz):
        base = pl.multiple_of(yx * DB, 16)
        return [(None, weight.at[core, z, pl.ds(base, DB), :])]

    return target


def run_copies(core, plans):
    for c in range(2):

        @pl.when(core == c)
        def _():
            for copy in plans[c]:
                copy.start()
            for copy in plans[c]:
                copy.wait()


def attention_forward(
    idx, x_ref, cos_ref, sin_ref, *rest
):
    mine, other = rest[0:5], rest[5:10]
    (
        weight, gain_ref, n1t_ref, qx_ref, kx_ref, kt_ref, vt_ref, ot_ref, lse_ref,
        y_ref, n2_ref, n2t_ref, gains, sems,
    ) = rest[10:]
    run_copies(idx[8], copies(idx, mine, other, sems, rows_target(weight, gains)))
    length = x_ref.shape[0]
    tiles = length // TILE
    first = idx[9]
    gain_one = jnp.concatenate([gains[b, 0:1, 0:DB] for b in range(QUAD)], axis=1).astype(F32)
    gain_two = jnp.concatenate([gains[b, 0:1, 256 : 256 + DB] for b in range(QUAD)], axis=1).astype(F32)
    gain_ref[0:1, :] = gain_one
    gain_ref[1:2, :] = gain_two

    place = lax.broadcasted_iota(jnp.int32, (HEAD_DIM, length), 1)
    row = lax.broadcasted_iota(jnp.int32, (HEAD_DIM, length), 0)
    extra_q = jnp.where((row == 0) & (place >= first), NEG, 0.0).astype(BF16)
    extra_k = jnp.where((row == 0) & (place < first), 1.0, 0.0)
    for h in range(HEADS):
        qx_ref[h, HEAD_DIM:, :] = extra_q

    def project(i, carry):
        at = pl.ds(pl.multiple_of(i * TILE, TILE), TILE)
        x = x_ref[at, :].astype(F32)
        inverse = lax.rsqrt(jnp.mean(x * x, axis=-1, keepdims=True) + EPS)
        n1 = x * inverse * gain_one
        n1b = n1.astype(BF16)
        n1t_ref[:, at] = n1b.T
        cosine, sine = cos_ref[:, at], sin_ref[:, at]
        flat = [nn(n1b, weight[z, :, LEAD:]).T for z in range(QUAD)]
        queries = jnp.concatenate([f[SKIP : SKIP + QB] for f in flat], axis=0)
        keys = jnp.concatenate([f[SKIP + QB : SKIP + QB + KB] for f in flat], axis=0)
        values = jnp.concatenate([f[SKIP + QB + KB :] for f in flat], axis=0)
        for h in range(HEADS):
            u1 = queries[h * HEAD_DIM : h * HEAD_DIM + HALF]
            u2 = queries[h * HEAD_DIM + HALF : (h + 1) * HEAD_DIM]
            turned = jnp.concatenate([u1 * cosine - u2 * sine, u2 * cosine + u1 * sine], axis=0)
            qx_ref[h, 0:HEAD_DIM, at] = turned.astype(BF16) * jnp.asarray(0.125, BF16)
        for h in range(KV_HEADS):
            u1 = keys[h * HEAD_DIM : h * HEAD_DIM + HALF]
            u2 = keys[h * HEAD_DIM + HALF : (h + 1) * HEAD_DIM]
            turned = jnp.concatenate([u1 * cosine - u2 * sine, u2 * cosine + u1 * sine], axis=0)
            kt_ref[h, :, at] = turned.astype(BF16)
        vt_ref[:, :, at] = values.astype(BF16).reshape(KV_HEADS, HEAD_DIM, TILE)
        return carry

    lax.fori_loop(0, tiles, project, 0)

    causal = lax.broadcasted_iota(jnp.int32, (TILE, GROUP * TILE), 0) > (
        lax.broadcasted_iota(jnp.int32, (TILE, GROUP * TILE), 1) % TILE
    )

    def head(j, carry):
        wide = jnp.concatenate([kt_ref[j].astype(F32), extra_k], axis=0)
        kx_ref[j] = wide.T.astype(BF16)
        for b in range(tiles):
            at = slice(b * TILE, (b + 1) * TILE)
            qx = jnp.concatenate([qx_ref[GROUP * j + g, :, at] for g in range(GROUP)], axis=1)
            scores = []
            for s in range(b + 1):
                raw = nn(kx_ref[j, s * TILE : (s + 1) * TILE, :], qx)
                scores.append(jnp.where(causal, NEG, raw) if s == b else raw)
            highest = functools.reduce(jnp.maximum, [jnp.max(s, axis=0, keepdims=True) for s in scores])
            total = 0.0
            out = 0.0
            for s in range(b + 1):
                weights = jnp.exp(scores[s] - highest)
                total = total + jnp.sum(weights, axis=0, keepdims=True)
                out = out + nn(vt_ref[j, :, s * TILE : (s + 1) * TILE], weights.astype(BF16))
            out = out / total
            lse_ref[j, b] = highest + jnp.log(total)
            for g in range(GROUP):
                ot_ref[GROUP * j + g, :, at] = out[:, g * TILE : (g + 1) * TILE].astype(BF16)
        return carry

    lax.fori_loop(0, KV_HEADS, head, 0)

    def finish(i, carry):
        at = pl.ds(pl.multiple_of(i * TILE, TILE), TILE)
        o = ot_ref[:, :, at].reshape(D, TILE).T
        added = jnp.concatenate([nn(o, weight[z, :, 0:256])[:, 0:DB] for z in range(QUAD)], axis=1)
        y = x_ref[at, :].astype(F32) + added
        y_ref[at, :] = y
        inverse = lax.rsqrt(jnp.mean(y * y, axis=-1, keepdims=True) + EPS)
        n2 = (y * inverse * gain_two).astype(BF16)
        n2_ref[at, :] = n2
        n2t_ref[:, at] = n2.T
        return carry

    lax.fori_loop(0, tiles, finish, 0)


def call_attention_forward(idx, x, cosine, sine, mine, other):
    length = x.shape[0]
    tiles = length // TILE
    s = jax.ShapeDtypeStruct
    vm = pl.BlockSpec(memory_space=pltpu.VMEM)
    return pl.pallas_call(
        attention_forward,
        out_shape=(
            s((QUAD, D, FB), BF16),
            s((8, D), F32),
            s((D, length), BF16),
            s((HEADS, 2 * HEAD_DIM, length), BF16),
            s((KV_HEADS, length, 2 * HEAD_DIM), BF16),
            s((KV_HEADS, HEAD_DIM, length), BF16),
            s((KV_HEADS, HEAD_DIM, length), BF16),
            s((HEADS, HEAD_DIM, length), BF16),
            s((KV_HEADS, tiles, 1, GROUP * TILE), F32),
            s((length, D), F32),
            s((length, D), BF16),
            s((D, length), BF16),
        ),
        in_specs=[pl.BlockSpec(memory_space=pltpu.SMEM)] + [vm] * 3 + [any_spec()] * 10,
        out_specs=(vm,) * 12,
        scratch_shapes=[
            pltpu.VMEM((QUAD, SPARE, FB), BF16),
            pltpu.SemaphoreType.DMA((64,)),
        ],
        compiler_params=params(),
        name="attention_forward",
        cost_estimate=pl.CostEstimate(flops=20_000_000_000, bytes_accessed=30_000_000, transcendentals=10_000_000),
    )(idx, x, cosine, sine, *mine, *other)


def feed(idx, n2_ref, y_ref, c_ref, gain_ref, *rest):
    pairs, downs = rest[0:10], rest[10:20]
    (
        mixed_ref, h_ref, dgu_ref, dy_ref, dat_ref, ct_ref, gg_ref,
        weight, down, gate, rise, sems,
    ) = rest[20:]

    @pl.when(pl.program_id(0) == 0)
    def _():
        first = copies(idx, pairs[0:5], pairs[5:10], sems.at[0], pair_target(weight))
        second = copies(idx, downs[0:5], downs[5:10], sems.at[1], down_target(down))
        run_copies(idx[8], [a + b for a, b in zip(first, second)])
        gg_ref[...] = jnp.zeros_like(gg_ref)

    n2 = n2_ref[...]
    for b in range(QUAD):
        at = slice(b * FB, (b + 1) * FB)
        g = nn(n2, weight[0, b])
        u = nn(n2, weight[1, b])
        gate[:, at] = g
        rise[:, at] = u
        h_ref[b] = (g / (1.0 + jnp.exp(-g)) * u).astype(BF16)
    y = y_ref[...]
    total = y
    for b in range(QUAD):
        total = total + nt(h_ref[b], down[b])
    mixed_ref[...] = total.astype(BF16)
    c = c_ref[...]
    ct_ref[...] = c.T
    dn2 = jnp.zeros((TILE, D), F32)
    for b in range(QUAD):
        at = slice(b * FB, (b + 1) * FB)
        dh = nn(c, down[b])
        g, u = gate[:, at], rise[:, at]
        sig = 1.0 / (1.0 + jnp.exp(-g))
        silu = g * sig
        dg = (dh * u * (sig + silu * (1.0 - sig))).astype(BF16)
        du = (dh * silu).astype(BF16)
        dgu_ref[0, b] = dg
        dgu_ref[1, b] = du
        dn2 = dn2 + nt(dg, weight[0, b]) + nt(du, weight[1, b])
    r = lax.rsqrt(jnp.mean(y * y, axis=-1, keepdims=True) + EPS)
    yr = y * r
    gg_ref[0:1, :] += jnp.sum(dn2 * yr, axis=0, keepdims=True)
    t = dn2 * gain_ref[1:2, :]
    dy = c.astype(F32) + r * (t - yr * jnp.mean(t * yr, axis=-1, keepdims=True))
    dy_ref[...] = dy
    dat_ref[...] = dy.astype(BF16).T


def call_feed(idx, n2, y, c, gains, pairs, downs):
    length = n2.shape[0]
    s = jax.ShapeDtypeStruct
    wide = pl.BlockSpec((TILE, D), lambda i, p: (i, 0))
    tall = pl.BlockSpec((D, TILE), lambda i, p: (0, i))
    whole = pl.BlockSpec((8, D), lambda i, p: (0, 0))
    return pl.pallas_call(
        feed,
        out_shape=(
            s((length, D), BF16),
            s((QUAD, length, FB), BF16),
            s((2, QUAD, length, FB), BF16),
            s((length, D), F32),
            s((D, length), BF16),
            s((D, length), BF16),
            s((8, D), F32),
        ),
        grid_spec=pltpu.PrefetchScalarGridSpec(
            num_scalar_prefetch=1,
            grid=(length // TILE,),
            in_specs=[wide, wide, wide, whole] + [any_spec()] * 20,
            out_specs=[
                wide,
                pl.BlockSpec((QUAD, TILE, FB), lambda i, p: (0, i, 0)),
                pl.BlockSpec((2, QUAD, TILE, FB), lambda i, p: (0, 0, i, 0)),
                wide,
                tall,
                tall,
                whole,
            ],
            scratch_shapes=[
                pltpu.VMEM((2, QUAD, D, FB), BF16),
                pltpu.VMEM((QUAD, D, FB), BF16),
                pltpu.VMEM((TILE, FF), F32),
                pltpu.VMEM((TILE, FF), F32),
                pltpu.SemaphoreType.DMA((2, 64)),
            ],
        ),
        compiler_params=params(),
        name="feed_forward_backward",
        cost_estimate=pl.CostEstimate(flops=30_000_000_000, bytes_accessed=50_000_000, transcendentals=5_000_000),
    )(idx, n2, y, c, gains, *pairs, *downs)


def pair_grads(target, idx, n2t_ref, d_ref, *rest):
    received, outs = (rest[0:1], rest[1:]) if len(rest) > 1 and target == 0 else ((), rest)
    for k in range(QUAD):
        rows = pl.ds(pl.multiple_of(idx[k] * DB, 16), DB)
        got = nn(n2t_ref[rows, :], d_ref[...])
        if received:
            got = got + received[0][k, 0].astype(F32)
        if len(outs) == 1:
            outs[0][k, 0] = got.astype(BF16)
        else:
            outs[k][0] = got.astype(BF16)


def call_pair_grads(idx, n2t, dgu, received=None):
    length = n2t.shape[1]
    s = jax.ShapeDtypeStruct
    block = pl.BlockSpec((QUAD, 1, DB, FB), lambda i, p: (0, i, 0, 0))
    matrix = 10 if received is None else 8
    specs = [
        pl.BlockSpec((D, length), lambda i, p: (0, 0)),
        pl.BlockSpec((None, None, length, FB), lambda i, p: (p[matrix], p[4 + i], 0, 0)),
    ]
    if received is None:
        out_shape = [s((QUAD, QUAD, DB, FB), BF16)]
        out_specs = [block]
        extra = ()
    else:
        specs.append(block)
        extra = (received,)
        out_shape = [s((QUAD, DB, FB), BF16)] * QUAD
        out_specs = [pl.BlockSpec((1, DB, FB), lambda i, p: (i, 0, 0))] * QUAD
    return pl.pallas_call(
        functools.partial(pair_grads, 1 if received is None else 0),
        out_shape=out_shape,
        grid_spec=pltpu.PrefetchScalarGridSpec(
            num_scalar_prefetch=1, grid=(QUAD,), in_specs=specs, out_specs=out_specs
        ),
        compiler_params=params(),
        name="pair_grads",
        cost_estimate=pl.CostEstimate(flops=5_000_000_000, bytes_accessed=15_000_000, transcendentals=0),
    )(idx, n2t, dgu, *extra)


WIDE = FB + 256


def down_grads(which, idx, ct_ref, h_ref, ot_ref, dat_ref, gg_ref, *rest):
    received, outs = (rest[0:1], rest[1:]) if which == 8 else ((), rest)
    core = idx[which]
    z = idx[4 + pl.program_id(0)]
    start = pl.multiple_of(z * DB + core * (DB - ROWS), 16)
    left = ct_ref[pl.ds(start, ROWS), :]
    right = dat_ref[pl.ds(pl.multiple_of(z * DB, 16), DB), :]
    for k in range(QUAD):
        yx = idx[k]
        got = nn(left, h_ref[yx])
        begin = pl.multiple_of(yx * DB + core * (DB - ROWS), 16)
        also = nt(ot_ref[pl.ds(begin, ROWS), :], right)
        spare = jnp.broadcast_to(gg_ref[yx, 0:1, :], (SPARE, FB))
        head = jnp.where(core == 1, spare, got[0:SPARE])
        if received:
            got = got + received[0][k, 0, :, 0:FB].astype(F32)
            also = also + received[0][k, 0, :, FB : FB + DB].astype(F32)
            head = head + received[0][k, 0, 0:SPARE, 0:FB].astype(F32)
            ref = outs[k].at[0]
        else:
            ref = outs[0].at[k, 0]
        ref[:, 0:FB] = got.astype(BF16)
        ref[:, FB : FB + DB] = also.astype(BF16)
        ref[:, FB + DB :] = jnp.zeros((ROWS, 256 - DB), BF16)
        ref[0:SPARE, 0:FB] = head.astype(BF16)


def call_down_grads(idx, ct, h, ot, dat, gg, received=None):
    length = ct.shape[1]
    s = jax.ShapeDtypeStruct
    block = pl.BlockSpec((QUAD, 1, ROWS, WIDE), lambda i, p: (0, i, 0, 0))
    vm = pl.BlockSpec((D, length), lambda i, p: (0, 0))
    specs = [
        vm,
        pl.BlockSpec(memory_space=pltpu.VMEM),
        vm,
        vm,
        pl.BlockSpec((QUAD, 8, FB), lambda i, p: (0, 0, 0)),
    ]
    if received is None:
        out_shape, out_specs, extra = [s((QUAD, QUAD, ROWS, WIDE), BF16)], [block], ()
    else:
        specs.append(block)
        extra = (received,)
        out_shape = [s((QUAD, ROWS, WIDE), BF16)] * QUAD
        out_specs = [pl.BlockSpec((1, ROWS, WIDE), lambda i, p: (i, 0, 0))] * QUAD
    return pl.pallas_call(
        functools.partial(down_grads, 10 if received is None else 8),
        out_shape=out_shape,
        grid_spec=pltpu.PrefetchScalarGridSpec(
            num_scalar_prefetch=1, grid=(QUAD,), in_specs=specs, out_specs=out_specs
        ),
        compiler_params=params(),
        name="down_grads",
        cost_estimate=pl.CostEstimate(flops=4_000_000_000, bytes_accessed=15_000_000, transcendentals=0),
    )(idx, ct, h, ot, dat, gg, *extra)


def attention_backward(
    idx, x_ref, gain_ref, weight, n1t_ref, qx_ref, kx_ref, kt_ref, vt_ref, ot_ref, lse_ref, dat_ref, dy_ref,
    cos_ref, sin_ref, gx_ref, z_ref, gg_ref, dot_s, zq, zk, zv, dk_s, dv_s,
):
    length = x_ref.shape[0]
    tiles = length // TILE

    def back(i, carry):
        at = pl.ds(pl.multiple_of(i * TILE, TILE), TILE)
        total = 0.0
        for z in range(QUAD):
            total = total + nn(weight[z, :, 0:DB], dat_ref[z * DB : (z + 1) * DB, at])
        dot_s[:, :, at] = total.astype(BF16).reshape(HEADS, HEAD_DIM, TILE)
        return carry

    lax.fori_loop(0, tiles, back, 0)

    causal = lax.broadcasted_iota(jnp.int32, (TILE, GROUP * TILE), 0) > (
        lax.broadcasted_iota(jnp.int32, (TILE, GROUP * TILE), 1) % TILE
    )

    def unrotate(grads, cosine, sine):
        u1, u2 = grads[:HALF], grads[HALF:]
        return jnp.concatenate([u1 * cosine + u2 * sine, u2 * cosine - u1 * sine], axis=0)

    def head(j, carry):
        values = vt_ref[j].astype(F32).T.astype(BF16)
        for b in range(tiles):
            at = slice(b * TILE, (b + 1) * TILE)
            qx = jnp.concatenate([qx_ref[GROUP * j + g, :, at] for g in range(GROUP)], axis=1)
            do = jnp.concatenate([dot_s[GROUP * j + g, :, at] for g in range(GROUP)], axis=1)
            o = jnp.concatenate([ot_ref[GROUP * j + g, :, at] for g in range(GROUP)], axis=1)
            inner = jnp.sum(do.astype(F32) * o.astype(F32), axis=0, keepdims=True)
            log_total = lse_ref[j, b]
            dq = 0.0
            for s in range(b + 1):
                keys = slice(s * TILE, (s + 1) * TILE)
                raw = nn(kx_ref[j, keys, :], qx)
                if s == b:
                    raw = jnp.where(causal, NEG, raw)
                probs = jnp.exp(raw - log_total)
                dp = nn(values[keys, :], do)
                ds = (probs * (dp - inner)).astype(BF16)
                dq = dq + nn(kt_ref[j, :, keys], ds)
                dk = nt(ds, qx[0:HEAD_DIM, :])
                dv = nt(probs.astype(BF16), do)
                if s == b:
                    dk_s[keys, :] = dk
                    dv_s[keys, :] = dv
                else:
                    dk_s[keys, :] += dk
                    dv_s[keys, :] += dv
            cosine, sine = cos_ref[:, at], sin_ref[:, at]
            for g in range(GROUP):
                part = unrotate(dq[:, g * TILE : (g + 1) * TILE] * 0.125, cosine, sine)
                zq[GROUP * j + g, :, at] = part.astype(BF16)
        zk[j] = unrotate(dk_s[...].T, cos_ref[...], sin_ref[...]).astype(BF16)
        zv[j] = dv_s[...].T.astype(BF16)
        return carry

    lax.fori_loop(0, KV_HEADS, head, 0)

    gain_one = gain_ref[0:1, :]
    for z in range(QUAD):
        z_ref[z, 0:SKIP, :] = jnp.zeros((SKIP, length), BF16)
    flat_q, flat_k, flat_v = (a.reshape(-1, length) for a in (zq, zk, zv))
    for z in range(QUAD):
        z_ref[z, SKIP : SKIP + QB, :] = flat_q[z * QB : (z + 1) * QB, :]
        z_ref[z, SKIP + QB : SKIP + QB + KB, :] = flat_k[z * KB : (z + 1) * KB, :]
        z_ref[z, SKIP + QB + KB :, :] = flat_v[z * KB : (z + 1) * KB, :]
    gg_ref[...] = jnp.zeros_like(gg_ref)

    def finish(i, carry):
        at = pl.ds(pl.multiple_of(i * TILE, TILE), TILE)
        total = 0.0
        for z in range(QUAD):
            total = total + nn(weight[z, :, LEAD:], z_ref[z, :, at])
        dn1 = total.T
        x = x_ref[at, :].astype(F32)
        r = lax.rsqrt(jnp.mean(x * x, axis=-1, keepdims=True) + EPS)
        xr = x * r
        gg_ref[0:1, :] += jnp.sum(dn1 * xr, axis=0, keepdims=True)
        t = dn1 * gain_one
        gx = dy_ref[at, :] + r * (t - xr * jnp.mean(t * xr, axis=-1, keepdims=True))
        gx_ref[at, :] = gx.astype(BF16)
        return carry

    lax.fori_loop(0, tiles, finish, 0)


def call_attention_backward(idx, *args):
    length = args[0].shape[0]
    s = jax.ShapeDtypeStruct
    vm = pl.BlockSpec(memory_space=pltpu.VMEM)
    return pl.pallas_call(
        attention_backward,
        out_shape=(
            s((length, D), BF16),
            s((QUAD, 512, length), BF16),
            s((8, D), F32),
        ),
        in_specs=[pl.BlockSpec(memory_space=pltpu.SMEM)] + [vm] * len(args),
        out_specs=(vm,) * 3,
        scratch_shapes=[
            pltpu.VMEM((HEADS, HEAD_DIM, length), BF16),
            pltpu.VMEM((HEADS, HEAD_DIM, length), BF16),
            pltpu.VMEM((KV_HEADS, HEAD_DIM, length), BF16),
            pltpu.VMEM((KV_HEADS, HEAD_DIM, length), BF16),
            pltpu.VMEM((length, HEAD_DIM), F32),
            pltpu.VMEM((length, HEAD_DIM), F32),
        ],
        compiler_params=params(),
        name="attention_backward",
        cost_estimate=pl.CostEstimate(flops=30_000_000_000, bytes_accessed=30_000_000, transcendentals=10_000_000),
    )(idx, *args)


def qkv_grads(which, idx, z_ref, n1t_ref, gg_ref, *rest):
    received, outs = (rest[0:1], rest[1:]) if which == 8 else ((), rest)
    core = idx[which]
    start = pl.multiple_of(SKIP + core * (QKV - QKV_ROWS), 16)
    left = z_ref[pl.ds(start, QKV_ROWS), :]
    for k in range(QUAD):
        yx = idx[k]
        got = nt(left, n1t_ref[pl.ds(pl.multiple_of(yx * DB, 16), DB), :])
        spare = jnp.broadcast_to(gg_ref[yx, 0:1, :], (SPARE, DB))
        head = jnp.where(core == 1, spare, got[0:SPARE])
        if received:
            got = got + received[0][k, 0].astype(F32)
            head = head + received[0][k, 0, 0:SPARE].astype(F32)
            ref = outs[k].at[0]
        else:
            ref = outs[0].at[k, 0]
        ref[...] = got.astype(BF16)
        ref[0:SPARE, :] = head.astype(BF16)


def call_qkv_grads(idx, z, n1t, gg, received=None):
    length = n1t.shape[1]
    s = jax.ShapeDtypeStruct
    block = pl.BlockSpec((QUAD, 1, QKV_ROWS, DB), lambda i, p: (0, i, 0, 0))
    specs = [
        pl.BlockSpec((None, 512, length), lambda i, p: (p[4 + i], 0, 0)),
        pl.BlockSpec((D, length), lambda i, p: (0, 0)),
        pl.BlockSpec((QUAD, 8, DB), lambda i, p: (0, 0, 0)),
    ]
    if received is None:
        out_shape, out_specs, extra = [s((QUAD, QUAD, QKV_ROWS, DB), BF16)], [block], ()
    else:
        specs.append(block)
        extra = (received,)
        out_shape = [s((QUAD, QKV_ROWS, DB), BF16)] * QUAD
        out_specs = [pl.BlockSpec((1, QKV_ROWS, DB), lambda i, p: (i, 0, 0))] * QUAD
    return pl.pallas_call(
        functools.partial(qkv_grads, 10 if received is None else 8),
        out_shape=out_shape,
        grid_spec=pltpu.PrefetchScalarGridSpec(
            num_scalar_prefetch=1, grid=(QUAD,), in_specs=specs, out_specs=out_specs
        ),
        compiler_params=params(),
        name="qkv_grads",
        cost_estimate=pl.CostEstimate(flops=3_000_000_000, bytes_accessed=10_000_000, transcendentals=0),
    )(idx, z, n1t, gg, *extra)


CORE = [(i, i ^ 1) for i in range(8)]
ALONG_X = [(i, i ^ 2) for i in range(8)]
ALONG_Y = [(i, i ^ 4) for i in range(8)]
ACROSS = [(i, i ^ 6) for i in range(8)]


def swap(values):
    return lax.ppermute(values, "fsdp", CORE)


def from_z(values, k):
    return lax.ppermute(values, "dp", [(j, (j - k) % QUAD) for j in range(QUAD)])


def to_z(values, k):
    return lax.ppermute(values, "dp", [(j, (j + k) % QUAD) for j in range(QUAD)])


def spread_z(piece):
    return jnp.stack([piece] + [from_z(piece, k) for k in range(1, QUAD)])


def spread_plane(own):
    by_x = lax.ppermute(own, "fsdp", ALONG_X)
    by_y = lax.ppermute(own, "fsdp", ALONG_Y)
    low = lax.ppermute(by_y[0:2], "fsdp", ALONG_X)
    high = lax.ppermute(by_x[2:4], "fsdp", ALONG_Y)
    return (own, by_x, by_y, low, high)


def spread_core(pieces):
    return tuple(swap(piece) for piece in pieces)


def add(parts):
    return functools.reduce(jnp.add, [part.astype(F32) for part in parts])


def sum_plane(blocks):
    got = (
        blocks[0],
        lax.ppermute(blocks[1], "fsdp", ALONG_X),
        lax.ppermute(blocks[2], "fsdp", ALONG_Y),
        lax.ppermute(blocks[3], "fsdp", ACROSS),
    )
    return add(got).astype(BF16)


def sum_z(blocks):
    return add([blocks[0]] + [to_z(blocks[k], k) for k in range(1, QUAD)])


def slab(values, start, size, axis):
    return lax.dynamic_slice_in_dim(values, start, size, axis)


def tables(yx, z, core, first):
    entries = [yx ^ k for k in range(QUAD)] + [(z + k) % QUAD for k in range(QUAD)]
    entries += [core, first, 1 - core, 0, 0, 0, 0, 0]
    return jnp.stack([jnp.asarray(e, jnp.int32) for e in entries])


def gather_near(core, gain_attn, w_query, w_key, w_value, w_out, gain_mlp, w_gate, w_up, w_down):
    zero = core == 0
    rows = jnp.concatenate([w_out, w_query, w_key, w_value], axis=1)
    share = rows.shape[0]
    extra = ROWS - share
    pad = jnp.zeros((1, 256 - DB), BF16)
    gains = jnp.concatenate(
        [gain_attn[None], jnp.zeros((1, 256 - share), BF16), gain_mlp[None], jnp.zeros((1, FB - 256 - share), BF16)], axis=1
    )
    sent = jnp.concatenate([rows[0:extra], gains, jnp.zeros((SPARE - extra - 1, FB), BF16)], axis=0)
    taken = swap(sent)
    theirs = taken[extra : extra + 1]
    line = jnp.concatenate(
        [theirs[:, 0:share], gain_attn[None], pad, theirs[:, 256 : 256 + share], gain_mlp[None], jnp.zeros((1, FB - 256 - DB), BF16)],
        axis=1,
    )
    attn = jnp.where(
        zero,
        jnp.concatenate([rows, taken[0:extra]], axis=0),
        jnp.concatenate([jnp.broadcast_to(line, (SPARE, FB)), rows[extra:]], axis=0),
    )
    attn = spread_z(attn)
    w_gate, w_up, w_down, attn = lax.optimization_barrier((w_gate, w_up, w_down, attn))
    taken = swap(jnp.where(zero, w_up, w_gate))
    pair = jnp.where(zero, jnp.concatenate([w_gate, taken], axis=0), jnp.concatenate([taken, w_up], axis=0))
    turned = w_down.T
    taken = swap(slab(turned, (1 - core) * (DB - ROWS), ROWS, 0))
    kept = slab(turned, core * (DB - ROWS), ROWS, 0)
    down = jnp.where(zero, jnp.concatenate([kept, taken], axis=1), jnp.concatenate([taken, kept], axis=1))
    attn = spread_plane(attn)
    attn_other = spread_core(attn)
    pair = spread_plane(spread_z(pair))
    pair_other = spread_core(pair)
    down = spread_plane(spread_z(down))
    down_other = spread_core(down)
    return attn + attn_other, pair + pair_other, down + down_other


def in_pieces(blocks):
    return (blocks[0], blocks[1], blocks[2], blocks[3, 0:2], blocks[3, 2:4])


def gather_any(gain_attn, w_query, w_key, w_value, w_out, gain_mlp, w_gate, w_up, w_down):
    def whole(weight):
        return lax.all_gather(lax.all_gather(weight, "dp", axis=1, tiled=True), "fsdp", axis=0, tiled=True)

    def blocks(weight):
        return weight.reshape(QUAD, weight.shape[0] // QUAD, QUAD, weight.shape[1] // QUAD).transpose(0, 2, 1, 3)

    attn = jnp.concatenate([blocks(whole(w)) for w in (w_out, w_query, w_key, w_value)], axis=3)
    gains = [lax.all_gather(g, "fsdp", axis=0, tiled=True).reshape(QUAD, 1, 1, DB) for g in (gain_attn, gain_mlp)]
    line = jnp.concatenate(
        [gains[0], jnp.zeros((QUAD, 1, 1, 256 - DB), BF16), gains[1], jnp.zeros((QUAD, 1, 1, FB - 256 - DB), BF16)], axis=3
    )
    line = jnp.broadcast_to(line, (QUAD, QUAD, SPARE, FB))
    attn_two = jnp.concatenate([line, attn[:, :, ROWS:]], axis=2)
    down = blocks(whole(w_down).T).transpose(1, 0, 2, 3)
    pair = [in_pieces(blocks(whole(w))) for w in (w_gate, w_up)]
    return (
        in_pieces(attn[:, :, 0:ROWS]) + in_pieces(attn_two),
        pair[0] + pair[1],
        in_pieces(down[:, :, 0:ROWS]) + in_pieces(down[:, :, DB - ROWS :]),
    )


def on_device(
    near,
    tokens,
    first_len,
    gain_attn,
    w_query,
    w_key,
    w_value,
    w_out,
    gain_mlp,
    w_gate,
    w_up,
    w_down,
    cotangent,
):
    length = tokens.shape[0]
    first = first_len[0]
    weights = (gain_attn, w_query, w_key, w_value, w_out, gain_mlp, w_gate, w_up, w_down)
    if near:
        place = lax.axis_index("fsdp")
        core = place & 1
        idx = tables(place >> 1, lax.axis_index("dp"), core, first)
        attn, pair, down = gather_near(core, *weights)
    else:
        idx = tables(0, 0, 0, first)
        attn, pair, down = gather_any(*weights)
    cosine, sine = rope_tables(first, length)
    (
        weight, gains, n1t, qx, kx, kt, vt, ot, lse, y, n2, n2t,
    ) = call_attention_forward(idx, tokens, cosine, sine, attn[0:5], attn[5:10])
    mixed, h, dgu, dy, dat, ct, gain_two = call_feed(idx, n2, y, cotangent, gains, pair, down)

    halves = gain_two[0].reshape(QUAD, 1, 2, DB // 2)
    row = jnp.pad(halves, ((0, 0), (0, 7), (0, 0), (0, FB // 2 - DB // 2))).reshape(QUAD, 8, FB)
    flat_o = ot.reshape(D, length)
    args_down = (ct, h, flat_o, dat, row)
    down_theirs = call_down_grads(idx, *args_down)[0]
    pair_theirs = call_pair_grads(idx, n2t, dgu)[0]
    if near:
        down_mine = call_down_grads(idx, *args_down, received=swap(down_theirs))
        pair_mine = call_pair_grads(idx, n2t, dgu, received=swap(pair_theirs))
        down_sum = sum_z(sum_plane(down_mine))
        pair_sum = sum_z(sum_plane(pair_mine))
    else:
        down_mine = call_down_grads(idx, *args_down, received=jnp.zeros_like(down_theirs))
        pair_mine = call_pair_grads(idx, n2t, dgu, received=jnp.zeros_like(pair_theirs))

    grad_tokens, turned, gain_one = call_attention_backward(
        idx, tokens, gains, weight, n1t, qx, kx, kt, vt, ot, lse, dat, dy, cosine, sine
    )
    row = jnp.pad(gain_one[0].reshape(QUAD, 1, DB), ((0, 0), (0, 7), (0, 0)))
    qkv_theirs = call_qkv_grads(idx, turned, n1t, row)[0]
    if near:
        qkv_mine = call_qkv_grads(idx, turned, n1t, row, received=swap(qkv_theirs))
        qkv_sum = sum_z(sum_plane(qkv_mine))
        outs = settle_near(core, down_sum, pair_sum, qkv_sum)
    else:
        qkv_mine = call_qkv_grads(idx, turned, n1t, row, received=jnp.zeros_like(qkv_theirs))
        outs = settle_any(down_mine, down_theirs, pair_mine, pair_theirs, qkv_mine, qkv_theirs, gain_one[0], gain_two[0])
    return (mixed, grad_tokens) + outs


def settle_near(core, down_sum, pair_sum, qkv_sum):
    zero = core == 0
    share = DB // 2

    kept = slab(pair_sum, core * share, share, 0)
    taken = swap(slab(pair_sum, (1 - core) * share, share, 0).astype(BF16)).astype(F32)
    grad_gate, grad_up = jnp.where(zero, kept, taken), jnp.where(zero, taken, kept)

    grad_out = jnp.where(zero, down_sum[0:share, FB : FB + DB], down_sum[ROWS - share :, FB : FB + DB])
    half = FB // 2
    kept = slab(down_sum, core * half, half, 1)
    taken = swap(slab(down_sum, (1 - core) * half, half, 1).astype(BF16)).astype(F32)
    upper, lower = jnp.where(zero, kept, taken), jnp.where(zero, taken, kept)
    grad_down = jnp.concatenate([upper, lower[SPARE:]], axis=0).T
    grad_gain_mlp = lower[0, 0:share]

    kept = slab(qkv_sum, core * share, share, 1)
    taken = swap(slab(qkv_sum, (1 - core) * share, share, 1).astype(BF16)).astype(F32)
    upper, lower = jnp.where(zero, kept, taken), jnp.where(zero, taken, kept)
    grad_gain_attn = lower[0]
    rows = jnp.concatenate([upper, lower[SPARE:]], axis=0).T
    return (
        grad_gain_attn, rows[:, 0:QB], rows[:, QB : QB + KB], rows[:, QB + KB :], grad_out,
        grad_gain_mlp, grad_gate, grad_up, grad_down,
    )


def settle_any(down_mine, down_theirs, pair_mine, pair_theirs, qkv_mine, qkv_theirs, gain_one, gain_two):
    def whole(blocks):
        return blocks.transpose(0, 2, 1, 3).reshape(blocks.shape[0] * blocks.shape[2], -1)

    def shard(values):
        values = lax.psum_scatter(values, "fsdp", scatter_dimension=0, tiled=True)
        return lax.psum_scatter(values, "dp", scatter_dimension=1, tiled=True).astype(F32)

    def gain(values):
        values = lax.psum(values, "dp")
        return lax.psum_scatter(values, "fsdp", scatter_dimension=0, tiled=True)

    both = jnp.concatenate([jnp.stack(down_mine), down_theirs[:, :, SPARE:]], axis=2)
    grad_down = shard(whole(both[..., 0:FB].transpose(1, 0, 2, 3)).T)
    grad_out = shard(whole(both[..., FB : FB + DB]))
    grad_gate, grad_up = shard(whole(jnp.stack(pair_mine))), shard(whole(pair_theirs))
    both = jnp.concatenate([jnp.stack(qkv_mine), qkv_theirs[:, :, SPARE:]], axis=2).transpose(0, 1, 3, 2)
    grad_query = shard(whole(both[..., 0:QB]))
    grad_key = shard(whole(both[..., QB : QB + KB]))
    grad_value = shard(whole(both[..., QB + KB :]))
    return (
        gain(gain_one), grad_query, grad_key, grad_value, grad_out, gain(gain_two), grad_gate, grad_up, grad_down,
    )


def solution(mesh):
    sizes = dict(mesh.shape)
    near = sizes["fsdp"] == 8 and sizes["dp"] == QUAD
    in_specs = (
        P(("fsdp", "dp"), None),
        P(("fsdp", "dp")),
        P("fsdp"),
        P("fsdp", "dp"),
        P("fsdp", "dp"),
        P("fsdp", "dp"),
        P("fsdp", "dp"),
        P("fsdp"),
        P("fsdp", "dp"),
        P("fsdp", "dp"),
        P("fsdp", "dp"),
        P(("fsdp", "dp"), None),
    )
    out_specs = (
        P(("fsdp", "dp"), None),
        P(("fsdp", "dp"), None),
        P("fsdp"),
        P("fsdp", "dp"),
        P("fsdp", "dp"),
        P("fsdp", "dp"),
        P("fsdp", "dp"),
        P("fsdp"),
        P("fsdp", "dp"),
        P("fsdp", "dp"),
        P("fsdp", "dp"),
    )
    return jax.shard_map(
        functools.partial(on_device, near), mesh=mesh, in_specs=in_specs, out_specs=out_specs, check_vma=False
    )
```

```python
import functools

import jax
import jax.numpy as jnp
from jax import lax
from jax.experimental import pallas as pl
from jax.experimental.pallas import tpu as pltpu
from jax.sharding import PartitionSpec as P

D = 960
FF = 2560
HEADS = 15
KV_HEADS = 5
GROUP = HEADS // KV_HEADS
HEAD_DIM = 64
HALF = HEAD_DIM // 2
TILE = 256
QUAD = 4
DB = D // QUAD
FB = FF // QUAD
QB = D // QUAD
KB = KV_HEADS * HEAD_DIM // QUAD
ROWS = 128
SPARE = 16
QKV = QB + 2 * KB
QKV_ROWS = 208
LEAD = FB - 512
SKIP = DB - LEAD
NEG = -1e30
EPS = 1e-05
ROPE_BASE = 10000.0
BIG = 60 * 1024 * 1024

F32 = jnp.float32
BF16 = jnp.bfloat16


def nn(a, b):
    return jnp.dot(a, b, preferred_element_type=F32)


def nt(a, b):
    return lax.dot_general(a, b, (((1,), (1,)), ((), ())), preferred_element_type=F32)


def rope_tables(first, length):
    places = jnp.arange(length, dtype=jnp.int32)
    position = jnp.where(places < first, places, places - first).astype(F32)
    frequency = ROPE_BASE ** (-jnp.arange(0, HEAD_DIM, 2, dtype=F32) / HEAD_DIM)
    angles = frequency[:, None] * position[None, :]
    return jnp.cos(angles), jnp.sin(angles)


def params():
    return pltpu.CompilerParams(vmem_limit_bytes=BIG)


def any_spec():
    return pl.BlockSpec(memory_space=pl.ANY)


def by_plane_halved(pieces, k, kz):
    if k < 3:
        return pieces[k].at[kz]
    return pieces[3 + kz // 2].at[kz % 2]


def by_z(pieces, k, kz):
    return pieces[kz].at[k]


def copies(idx, pieces, pick, sems, target):
    plans = ([], [])
    mine, other = pieces[: len(pieces) // 2], pieces[len(pieces) // 2 :]
    for mine_core in range(2):
        slot = 0
        for core, found in ((mine_core, mine), (1 - mine_core, other)):
            for k in range(QUAD):
                for kz in range(QUAD):
                    ref = pick(found, k, kz)
                    for source, dest in target(core, idx[4 + kz], idx[k], kz):
                        src = ref if source is None else ref.at[pl.ds(*source), :]
                        plans[mine_core].append(
                            pltpu.make_async_copy(src, dest, sems.at[slot])
                        )
                        slot += 1
    return plans


def rows_target(weight, gains=None):
    def target(core, z, yx, kz):
        base = pl.multiple_of(yx * DB, 16)
        if core == 0:
            return [((0, ROWS), weight.at[z, pl.ds(base, ROWS), :])]
        found = [((SPARE, DB - ROWS), weight.at[z, pl.ds(base + ROWS, DB - ROWS), :])]
        if gains is not None and kz == 0:
            found.append(((0, SPARE), gains.at[yx]))
        return found

    return target


def down_target(weight):
    def target(core, z, yx, kz):
        base = pl.multiple_of(z * DB, 16)
        columns = pl.ds(pl.multiple_of(yx * FB, 128), FB)
        if core == 0:
            return [((0, ROWS), weight.at[pl.ds(base, ROWS), columns])]
        return [((SPARE, DB - ROWS), weight.at[pl.ds(base + ROWS, DB - ROWS), columns])]

    return target


def pair_target(weight):
    def target(core, z, yx, kz):
        base = pl.multiple_of(yx * DB, 16)
        columns = pl.ds(pl.multiple_of(z * FB, 128), FB)
        return [(None, weight.at[core, pl.ds(base, DB), columns])]

    return target


def run_copies(core, plans):
    for c in range(2):

        @pl.when(core == c)
        def _():
            for copy in plans[c]:
                copy.start()
            for copy in plans[c]:
                copy.wait()


def norm_columns(x, axis):
    return lax.rsqrt(jnp.mean(x * x, axis=axis, keepdims=True) + EPS)


def column(row):
    return jnp.broadcast_to(row, (128, row.shape[1])).T[:, 0:1]


def project(idx, xt_ref, cos_ref, sin_ref, *rest):
    weight, gain_ref, n1t_ref, qx_ref, kx_ref, kt_ref, vt_ref, gains, sems = rest[10:]
    run_copies(idx[8], copies(idx, rest[0:10], by_plane_halved, sems, rows_target(weight, gains)))
    length = xt_ref.shape[1]
    first = idx[9]
    gain_one = jnp.concatenate([gains[b, 0:1, 0:DB] for b in range(QUAD)], axis=1).astype(F32)
    gain_two = jnp.concatenate([gains[b, 0:1, 256 : 256 + DB] for b in range(QUAD)], axis=1).astype(F32)
    gain_ref[0:1, :] = gain_one
    gain_ref[1:2, :] = gain_two
    gain_column = column(gain_one)

    place = lax.broadcasted_iota(jnp.int32, (HEAD_DIM, length), 1)
    row = lax.broadcasted_iota(jnp.int32, (HEAD_DIM, length), 0)
    extra_q = jnp.where((row == 0) & (place >= first), NEG, 0.0).astype(BF16)
    extra_k = jnp.where((row == 0) & (place < first), 1.0, 0.0)
    for h in range(HEADS):
        qx_ref[h, HEAD_DIM:, :] = extra_q

    def tile(i, carry):
        at = pl.ds(pl.multiple_of(i * TILE, TILE), TILE)
        x = xt_ref[:, at].astype(F32)
        n1t = (x * norm_columns(x, 0) * gain_column).astype(BF16)
        n1t_ref[:, at] = n1t
        n1 = n1t.T
        cosine, sine = cos_ref[:, at], sin_ref[:, at]
        flat = [nn(n1, weight[z, :, LEAD:]).T for z in range(QUAD)]
        queries = jnp.concatenate([f[SKIP : SKIP + QB] for f in flat], axis=0)
        keys = jnp.concatenate([f[SKIP + QB : SKIP + QB + KB] for f in flat], axis=0)
        values = jnp.concatenate([f[SKIP + QB + KB :] for f in flat], axis=0)

        def turn(u):
            u1, u2 = u[:HALF], u[HALF:]
            return jnp.concatenate([u1 * cosine - u2 * sine, u2 * cosine + u1 * sine], axis=0).astype(BF16)

        for h in range(HEADS):
            qx_ref[h, 0:HEAD_DIM, at] = turn(queries[h * HEAD_DIM : (h + 1) * HEAD_DIM]) * jnp.asarray(0.125, BF16)
        for h in range(KV_HEADS):
            kt_ref[h, :, at] = turn(keys[h * HEAD_DIM : (h + 1) * HEAD_DIM])
        vt_ref[:, :, at] = values.astype(BF16).reshape(KV_HEADS, HEAD_DIM, TILE)
        return carry

    lax.fori_loop(0, length // TILE, tile, 0)
    for j in range(KV_HEADS):
        wide = jnp.concatenate([kt_ref[j].astype(F32), extra_k], axis=0)
        kx_ref[j] = wide.T.astype(BF16)


def call_project(idx, xt, cosine, sine, pieces):
    length = xt.shape[1]
    s = jax.ShapeDtypeStruct
    vm = pl.BlockSpec(memory_space=pltpu.VMEM)
    return pl.pallas_call(
        project,
        out_shape=(
            s((QUAD, D, FB), BF16),
            s((8, D), F32),
            s((D, length), BF16),
            s((HEADS, 2 * HEAD_DIM, length), BF16),
            s((KV_HEADS, length, 2 * HEAD_DIM), BF16),
            s((KV_HEADS, HEAD_DIM, length), BF16),
            s((KV_HEADS, HEAD_DIM, length), BF16),
        ),
        in_specs=[pl.BlockSpec(memory_space=pltpu.SMEM)] + [vm] * 3 + [any_spec()] * 10,
        out_specs=(vm,) * 7,
        scratch_shapes=[
            pltpu.VMEM((QUAD, SPARE, FB), BF16),
            pltpu.SemaphoreType.DMA((64,)),
        ],
        compiler_params=params(),
        name="project",
        cost_estimate=pl.CostEstimate(flops=600000000, bytes_accessed=2000000, transcendentals=0),
    )(idx, xt, cosine, sine, *pieces)


def causal_mask():
    return lax.broadcasted_iota(jnp.int32, (TILE, GROUP * TILE), 0) > (
        lax.broadcasted_iota(jnp.int32, (TILE, GROUP * TILE), 1) % TILE
    )


def attend(qx_ref, kx_ref, vt_ref, ot_ref, lse_ref):
    tiles = qx_ref.shape[2] // TILE
    causal = causal_mask()
    for b in range(tiles):
        at = slice(b * TILE, (b + 1) * TILE)
        qx = jnp.concatenate([qx_ref[g, :, at] for g in range(GROUP)], axis=1)
        scores = []
        for s in range(b + 1):
            raw = nn(kx_ref[0, s * TILE : (s + 1) * TILE, :], qx)
            scores.append(jnp.where(causal, NEG, raw) if s == b else raw)
        highest = functools.reduce(jnp.maximum, [jnp.max(s, axis=0, keepdims=True) for s in scores])
        total = 0.0
        out = 0.0
        for s in range(b + 1):
            weights = jnp.exp(scores[s] - highest)
            total = total + jnp.sum(weights, axis=0, keepdims=True)
            out = out + nn(vt_ref[0, :, s * TILE : (s + 1) * TILE], weights.astype(BF16))
        out = out / total
        lse_ref[0, b] = highest + jnp.log(total)
        for g in range(GROUP):
            ot_ref[g, :, at] = out[:, g * TILE : (g + 1) * TILE].astype(BF16)


def heads_spec(count, rows, length):
    return pl.BlockSpec((count, rows, length), lambda j: (j, 0, 0))


def call_attend(qx, kx, vt):
    length = qx.shape[2]
    tiles = length // TILE
    s = jax.ShapeDtypeStruct
    return pl.pallas_call(
        attend,
        out_shape=(
            s((HEADS, HEAD_DIM, length), BF16),
            s((KV_HEADS, tiles, 1, GROUP * TILE), F32),
        ),
        grid=(KV_HEADS,),
        in_specs=[
            heads_spec(GROUP, 2 * HEAD_DIM, length),
            heads_spec(1, length, 2 * HEAD_DIM),
            heads_spec(1, HEAD_DIM, length),
        ],
        out_specs=[
            heads_spec(GROUP, HEAD_DIM, length),
            pl.BlockSpec((1, tiles, 1, GROUP * TILE), lambda j: (j, 0, 0, 0)),
        ],
        compiler_params=params(),
        name="attend",
        cost_estimate=pl.CostEstimate(flops=2000000000, bytes_accessed=800000, transcendentals=0),
    )(qx, kx, vt)


def leave(xt_ref, gain_ref, weight, ot_ref, y_ref, n2_ref, n2t_ref):
    o = ot_ref[...].reshape(D, ot_ref.shape[2]).T
    added = jnp.concatenate([nn(o, weight[z, :, 0:256])[:, 0:DB] for z in range(QUAD)], axis=1)
    y = xt_ref[...].T.astype(F32) + added
    y_ref[...] = y
    n2 = (y * norm_columns(y, -1) * gain_ref[1:2, :]).astype(BF16)
    n2_ref[...] = n2
    n2t_ref[...] = n2.T


def call_leave(xt, gains, weight, ot):
    length = xt.shape[1]
    s = jax.ShapeDtypeStruct
    tall = pl.BlockSpec((D, TILE), lambda i: (0, i))
    wide = pl.BlockSpec((TILE, D), lambda i: (i, 0))
    return pl.pallas_call(
        leave,
        out_shape=(s((length, D), F32), s((length, D), BF16), s((D, length), BF16)),
        grid=(length // TILE,),
        in_specs=[
            tall,
            pl.BlockSpec((8, D), lambda i: (0, 0)),
            pl.BlockSpec((QUAD, D, FB), lambda i: (0, 0, 0)),
            pl.BlockSpec((HEADS, HEAD_DIM, TILE), lambda i: (0, 0, i)),
        ],
        out_specs=[wide, wide, tall],
        compiler_params=params(),
        name="leave",
        cost_estimate=pl.CostEstimate(flops=300000000, bytes_accessed=1500000, transcendentals=0),
    )(xt, gains, weight, ot)


def feed(idx, n2_ref, y_ref, ct_ref, gain_ref, *rest):
    pairs, downs = rest[0:10], rest[10:18]
    mixed_ref, h_ref, dgu_ref, dyt_ref, dat_ref, gg_ref, weight, down, sems = rest[18:]

    @pl.when(pl.program_id(0) == 0)
    def _():
        first = copies(idx, pairs, by_plane_halved, sems.at[0], pair_target(weight))
        second = copies(idx, downs, by_z, sems.at[1], down_target(down))
        run_copies(idx[8], [a + b for a, b in zip(first, second)])
        gg_ref[...] = jnp.zeros_like(gg_ref)

    n2 = n2_ref[...]
    chunks = [slice(b, b + FEED_CHUNK) for b in range(0, FF, FEED_CHUNK)]
    for at in chunks:
        g = nn(n2, weight[0, :, at])
        u = nn(n2, weight[1, :, at])
        sig = 1.0 / (1.0 + jnp.exp(-g))
        silu = g * sig
        h_ref[:, at] = (silu * u).astype(BF16)
        dgu_ref[0, :, at] = (u * (sig + silu * (1.0 - sig))).astype(BF16)
        dgu_ref[1, :, at] = silu.astype(BF16)
    y = y_ref[...]
    mixed_ref[...] = (y + nt(h_ref[...], down[...])).astype(BF16).T
    c = ct_ref[...].T
    for at in chunks:
        dh = nn(c, down[:, at])
        dgu_ref[0, :, at] = (dh * dgu_ref[0, :, at].astype(F32)).astype(BF16)
        dgu_ref[1, :, at] = (dh * dgu_ref[1, :, at].astype(F32)).astype(BF16)
    dn2 = nt(dgu_ref[0], weight[0]) + nt(dgu_ref[1], weight[1])
    r = norm_columns(y, -1)
    yr = y * r
    gg_ref[0:1, :] += jnp.sum(dn2 * yr, axis=0, keepdims=True)
    t = dn2 * gain_ref[1:2, :]
    dy = c.astype(F32) + r * (t - yr * jnp.mean(t * yr, axis=-1, keepdims=True))
    dyt = dy.T
    dyt_ref[...] = dyt
    dat_ref[...] = dyt.astype(BF16)


FEED_TILE = 512
FEED_CHUNK = 512


def call_feed(idx, n2, y, ct, gains, pairs, downs):
    length = n2.shape[0]
    s = jax.ShapeDtypeStruct
    wide = pl.BlockSpec((FEED_TILE, D), lambda i, p: (i, 0))
    tall = pl.BlockSpec((D, FEED_TILE), lambda i, p: (0, i))
    whole = pl.BlockSpec((8, D), lambda i, p: (0, 0))
    return pl.pallas_call(
        feed,
        out_shape=(
            s((D, length), BF16),
            s((length, FF), BF16),
            s((2, length, FF), BF16),
            s((D, length), F32),
            s((D, length), BF16),
            s((8, D), F32),
        ),
        grid_spec=pltpu.PrefetchScalarGridSpec(
            num_scalar_prefetch=1,
            grid=(length // FEED_TILE,),
            in_specs=[wide, wide, tall, whole] + [any_spec()] * 18,
            out_specs=[
                tall,
                pl.BlockSpec((FEED_TILE, FF), lambda i, p: (i, 0)),
                pl.BlockSpec((2, FEED_TILE, FF), lambda i, p: (0, i, 0)),
                tall,
                tall,
                whole,
            ],
            scratch_shapes=[
                pltpu.VMEM((2, D, FF), BF16),
                pltpu.VMEM((D, FF), BF16),
                pltpu.SemaphoreType.DMA((2, 64)),
            ],
        ),
        compiler_params=params(),
        name="feed_forward_backward",
        cost_estimate=pl.CostEstimate(flops=3000000000, bytes_accessed=5000000, transcendentals=0),
    )(idx, n2, y, ct, gains, *pairs, *downs)


def pair_grads(target, idx, n2t_ref, d_ref, *rest):
    full = rest[-1]
    received, outs = (rest[0:1], rest[1:-1]) if target == 0 else ((), rest[:-1])
    full[...] = nn(n2t_ref[...], d_ref[...])
    for k in range(QUAD):
        got = full[pl.ds(pl.multiple_of(idx[k] * DB, 16), DB), :]
        if received:
            got = got + received[0][k, 0].astype(F32)
        if len(outs) == 1:
            outs[0][k, 0] = got.astype(BF16)
        else:
            outs[k][0] = got.astype(BF16)


def call_pair_grads(idx, n2t, dgu, received=None):
    length = n2t.shape[1]
    s = jax.ShapeDtypeStruct
    block = pl.BlockSpec((QUAD, 1, DB, FB), lambda i, p: (0, i, 0, 0))
    matrix = 10 if received is None else 8
    specs = [
        pl.BlockSpec((D, length), lambda i, p: (0, 0)),
        pl.BlockSpec((None, length, FB), lambda i, p: (p[matrix], 0, p[4 + i])),
    ]
    if received is None:
        out_shape = [s((QUAD, QUAD, DB, FB), BF16)]
        out_specs = [block]
        extra = ()
    else:
        specs.append(block)
        extra = (received,)
        out_shape = [s((QUAD, DB, FB), BF16)] * QUAD
        out_specs = [pl.BlockSpec((1, DB, FB), lambda i, p: (i, 0, 0))] * QUAD
    return pl.pallas_call(
        functools.partial(pair_grads, 1 if received is None else 0),
        out_shape=out_shape,
        grid_spec=pltpu.PrefetchScalarGridSpec(
            num_scalar_prefetch=1,
            grid=(QUAD,),
            in_specs=specs,
            out_specs=out_specs,
            scratch_shapes=[pltpu.VMEM((D, FB), F32)],
        ),
        compiler_params=params(),
        name="pair_grads",
        cost_estimate=pl.CostEstimate(flops=500000000, bytes_accessed=1500000, transcendentals=0),
    )(idx, n2t, dgu, *extra)


WIDE = FB + 256


def down_grads(which, idx, ct_ref, h_ref, ot_ref, dat_ref, gg_ref, *rest):
    right, also = rest[-2:]
    received, outs = (rest[0:1], rest[1:-2]) if which == 8 else ((), rest[:-2])
    core = idx[which]
    k = pl.program_id(0)
    yx = idx[k]
    offset = core * (DB - ROWS)

    def rows(ref, block, size, shift):
        return ref[pl.ds(pl.multiple_of(block * DB + shift, 16), size), :]

    @pl.when(k == 0)
    def _():
        for kz in range(QUAD):
            right[kz * DB : (kz + 1) * DB, :] = rows(dat_ref, idx[4 + kz], DB, 0)
        left = jnp.concatenate([rows(ot_ref, idx[i], ROWS, offset) for i in range(QUAD)], axis=0)
        also[...] = nt(left, right[...]).reshape(QUAD, ROWS, D)

    left = jnp.concatenate([rows(ct_ref, idx[4 + kz], ROWS, offset) for kz in range(QUAD)], axis=0)
    full = nn(left, h_ref[...])
    spare = jnp.broadcast_to(gg_ref[yx, 0:1, :], (SPARE, FB))

    def put(ref, kz):
        got = full[kz * ROWS : (kz + 1) * ROWS]
        out = also[k, :, kz * DB : (kz + 1) * DB]
        head = jnp.where(core == 1, spare, got[0:SPARE])
        if received:
            got = got + received[0][0, kz, :, 0:FB].astype(F32)
            out = out + received[0][0, kz, :, FB : FB + DB].astype(F32)
            head = head + received[0][0, kz, 0:SPARE, 0:FB].astype(F32)
        ref[:, 0:FB] = got.astype(BF16)
        ref[:, FB : FB + DB] = out.astype(BF16)
        ref[:, FB + DB :] = jnp.zeros((ROWS, 256 - DB), BF16)
        ref[0:SPARE, 0:FB] = head.astype(BF16)

    if len(outs) == 1:
        for kz in range(QUAD):
            put(outs[0].at[0, kz], kz)
    else:
        for i in range(QUAD):

            @pl.when(k == i)
            def _():
                for kz in range(QUAD):
                    put(outs[i].at[kz], kz)


def call_down_grads(idx, ct, h, ot, dat, gg, received=None):
    length = ct.shape[1]
    s = jax.ShapeDtypeStruct
    block = pl.BlockSpec((1, QUAD, ROWS, WIDE), lambda i, p: (i, 0, 0, 0))
    vm = pl.BlockSpec((D, length), lambda i, p: (0, 0))
    specs = [
        vm,
        pl.BlockSpec((length, FB), lambda i, p: (0, p[i])),
        vm,
        vm,
        pl.BlockSpec((QUAD, 8, FB), lambda i, p: (0, 0, 0)),
    ]
    if received is None:
        out_shape, out_specs, extra = [s((QUAD, QUAD, ROWS, WIDE), BF16)], [block], ()
    else:
        specs.append(block)
        extra = (received,)
        out_shape = [s((QUAD, ROWS, WIDE), BF16)] * QUAD
        out_specs = [pl.BlockSpec((QUAD, ROWS, WIDE), lambda i, p: (0, 0, 0))] * QUAD
    return pl.pallas_call(
        functools.partial(down_grads, 10 if received is None else 8),
        out_shape=out_shape,
        grid_spec=pltpu.PrefetchScalarGridSpec(
            num_scalar_prefetch=1,
            grid=(QUAD,),
            in_specs=specs,
            out_specs=out_specs,
            scratch_shapes=[pltpu.VMEM((D, length), BF16), pltpu.VMEM((QUAD, ROWS, D), F32)],
        ),
        compiler_params=params(),
        name="down_grads",
        cost_estimate=pl.CostEstimate(flops=400000000, bytes_accessed=1500000, transcendentals=0),
    )(idx, ct, h, ot, dat, gg, *extra)


def give(weight, dat_ref, do_ref):
    total = 0.0
    for z in range(QUAD):
        total = total + nn(weight[z, :, 0:DB], dat_ref[z * DB : (z + 1) * DB, :])
    do_ref[...] = total.astype(BF16).reshape(do_ref.shape)


def call_give(weight, dat):
    length = dat.shape[1]
    return pl.pallas_call(
        give,
        out_shape=jax.ShapeDtypeStruct((HEADS, HEAD_DIM, length), BF16),
        grid=(length // FEED_TILE,),
        in_specs=[
            pl.BlockSpec((QUAD, D, 256), lambda i: (0, 0, 0)),
            pl.BlockSpec((D, FEED_TILE), lambda i: (0, i)),
        ],
        out_specs=pl.BlockSpec((HEADS, HEAD_DIM, FEED_TILE), lambda i: (0, 0, i)),
        compiler_params=params(),
        name="give",
        cost_estimate=pl.CostEstimate(flops=200000000, bytes_accessed=600000, transcendentals=0),
    )(weight, dat)


def unrotate(grads, cosine, sine):
    u1, u2 = grads[:HALF], grads[HALF:]
    return jnp.concatenate([u1 * cosine + u2 * sine, u2 * cosine - u1 * sine], axis=0)


def attend_backward(qx_ref, kx_ref, kt_ref, vt_ref, ot_ref, do_ref, lse_ref, cos_ref, sin_ref, zq, zk, zv, dk_s, dv_s):
    tiles = qx_ref.shape[2] // TILE
    causal = causal_mask()
    values = vt_ref[0].astype(F32).T.astype(BF16)
    for b in range(tiles):
        at = slice(b * TILE, (b + 1) * TILE)
        qx = jnp.concatenate([qx_ref[g, :, at] for g in range(GROUP)], axis=1)
        do = jnp.concatenate([do_ref[g, :, at] for g in range(GROUP)], axis=1)
        o = jnp.concatenate([ot_ref[g, :, at] for g in range(GROUP)], axis=1)
        inner = jnp.sum(do.astype(F32) * o.astype(F32), axis=0, keepdims=True)
        log_total = lse_ref[0, b]
        dq = 0.0
        for s in range(b + 1):
            keys = slice(s * TILE, (s + 1) * TILE)
            raw = nn(kx_ref[0, keys, :], qx)
            if s == b:
                raw = jnp.where(causal, NEG, raw)
            probs = jnp.exp(raw - log_total)
            dp = nn(values[keys, :], do)
            ds = (probs * (dp - inner)).astype(BF16)
            dq = dq + nn(kt_ref[0, :, keys], ds)
            dk = nt(ds, qx[0:HEAD_DIM, :])
            dv = nt(probs.astype(BF16), do)
            if s == b:
                dk_s[keys, :] = dk
                dv_s[keys, :] = dv
            else:
                dk_s[keys, :] += dk
                dv_s[keys, :] += dv
        cosine, sine = cos_ref[:, at], sin_ref[:, at]
        for g in range(GROUP):
            part = unrotate(dq[:, g * TILE : (g + 1) * TILE] * 0.125, cosine, sine)
            zq[g, :, at] = part.astype(BF16)
    zk[0] = unrotate(dk_s[...].T, cos_ref[...], sin_ref[...]).astype(BF16)
    zv[0] = dv_s[...].T.astype(BF16)


def call_attend_backward(start, count, qx, kx, kt, vt, ot, do, lse, cosine, sine):
    length = qx.shape[2]
    tiles = length // TILE
    s = jax.ShapeDtypeStruct

    def spec(heads, rows, lanes):
        return pl.BlockSpec((heads, rows, lanes), lambda j: (j + start, 0, 0))

    table = pl.BlockSpec((HALF, length), lambda j: (0, 0))
    return pl.pallas_call(
        attend_backward,
        out_shape=(
            s((GROUP * count, HEAD_DIM, length), BF16),
            s((count, HEAD_DIM, length), BF16),
            s((count, HEAD_DIM, length), BF16),
        ),
        grid=(count,),
        in_specs=[
            spec(GROUP, 2 * HEAD_DIM, length),
            spec(1, length, 2 * HEAD_DIM),
            spec(1, HEAD_DIM, length),
            spec(1, HEAD_DIM, length),
            spec(GROUP, HEAD_DIM, length),
            spec(GROUP, HEAD_DIM, length),
            pl.BlockSpec((1, tiles, 1, GROUP * TILE), lambda j: (j + start, 0, 0, 0)),
            table,
            table,
        ],
        out_specs=[
            heads_spec(GROUP, HEAD_DIM, length),
            heads_spec(1, HEAD_DIM, length),
            heads_spec(1, HEAD_DIM, length),
        ],
        scratch_shapes=[pltpu.VMEM((length, HEAD_DIM), F32), pltpu.VMEM((length, HEAD_DIM), F32)],
        compiler_params=params(),
        name="attend_backward",
        cost_estimate=pl.CostEstimate(flops=1000000000, bytes_accessed=1000000, transcendentals=0),
    )(qx, kx, kt, vt, ot, do, lse, cosine, sine)


def enter_backward(xt_ref, dyt_ref, gain_ref, weight, *rest):
    parts, (gx_ref, z_ref, gg_ref, sums) = rest[:-4], rest[-4:]
    i = pl.program_id(0)

    @pl.when(i == 0)
    def _():
        sums[...] = jnp.zeros_like(sums)

    def flat(found):
        return jnp.concatenate([ref[...].reshape(-1, TILE) for ref in found], axis=0)

    zq, zk, zv = flat(parts[0::3]), flat(parts[1::3]), flat(parts[2::3])
    dn1 = 0.0
    for z in range(QUAD):
        z_ref[z, 0:SKIP, :] = jnp.zeros((SKIP, TILE), BF16)
        z_ref[z, SKIP : SKIP + QB, :] = zq[z * QB : (z + 1) * QB]
        z_ref[z, SKIP + QB : SKIP + QB + KB, :] = zk[z * KB : (z + 1) * KB]
        z_ref[z, SKIP + QB + KB :, :] = zv[z * KB : (z + 1) * KB]
        dn1 = dn1 + nn(weight[z, :, LEAD:], z_ref[z])
    x = xt_ref[...].astype(F32)
    r = norm_columns(x, 0)
    xr = x * r
    found = dn1 * xr
    sums[...] += found[:, 0:128] + found[:, 128:256]
    t = dn1 * column(gain_ref[0:1, :])
    gx = dyt_ref[...] + r * (t - xr * jnp.mean(t * xr, axis=0, keepdims=True))
    gx_ref[...] = gx.astype(BF16)

    @pl.when(i == pl.num_programs(0) - 1)
    def _():
        gg_ref[...] = jnp.broadcast_to(jnp.sum(sums[...].T, axis=0, keepdims=True), gg_ref.shape)


def call_enter_backward(xt, dyt, gains, weight, *parts):
    length = xt.shape[1]
    s = jax.ShapeDtypeStruct
    tall = pl.BlockSpec((D, TILE), lambda i: (0, i))
    whole = pl.BlockSpec((8, D), lambda i: (0, 0))
    return pl.pallas_call(
        enter_backward,
        out_shape=(s((D, length), BF16), s((QUAD, 512, length), BF16), s((8, D), F32)),
        grid=(length // TILE,),
        in_specs=[tall, tall, whole, pl.BlockSpec((QUAD, D, FB), lambda i: (0, 0, 0))]
        + [pl.BlockSpec((part.shape[0], HEAD_DIM, TILE), lambda i: (0, 0, i)) for part in parts],
        out_specs=[tall, pl.BlockSpec((QUAD, 512, TILE), lambda i: (0, 0, i)), whole],
        scratch_shapes=[pltpu.VMEM((D, 128), F32)],
        compiler_params=params(),
        name="enter_backward",
        cost_estimate=pl.CostEstimate(flops=400000000, bytes_accessed=1500000, transcendentals=0),
    )(xt, dyt, gains, weight, *parts)


def qkv_grads(idx, z_ref, n1t_ref, gg_ref, theirs, *rest):
    mine, (right, full) = rest[0:QUAD], rest[QUAD:]

    @pl.when(pl.program_id(0) == 0)
    def _():
        for k in range(QUAD):
            right[k * DB : (k + 1) * DB, :] = n1t_ref[pl.ds(pl.multiple_of(idx[k] * DB, 16), DB), :]

    full[...] = nt(z_ref[SKIP:, :], right[...])
    for which in (10, 8):
        core = idx[which]
        part = full[pl.ds(pl.multiple_of(core * (QKV - QKV_ROWS), 16), QKV_ROWS), :]
        for k in range(QUAD):
            got = part[:, k * DB : (k + 1) * DB]
            spare = jnp.broadcast_to(gg_ref[idx[k], 0:1, :], (SPARE, DB))
            ref = theirs.at[k, 0] if which == 10 else mine[k].at[0]
            ref[...] = got.astype(BF16)
            ref[0:SPARE, :] = jnp.where(core == 1, spare, got[0:SPARE]).astype(BF16)


def call_qkv_grads(idx, z, n1t, gg):
    length = n1t.shape[1]
    s = jax.ShapeDtypeStruct
    return pl.pallas_call(
        qkv_grads,
        out_shape=[s((QUAD, QUAD, QKV_ROWS, DB), BF16)] + [s((QUAD, QKV_ROWS, DB), BF16)] * QUAD,
        grid_spec=pltpu.PrefetchScalarGridSpec(
            num_scalar_prefetch=1,
            grid=(QUAD,),
            in_specs=[
                pl.BlockSpec((None, 512, length), lambda i, p: (p[4 + i], 0, 0)),
                pl.BlockSpec((D, length), lambda i, p: (0, 0)),
                pl.BlockSpec((QUAD, 8, DB), lambda i, p: (0, 0, 0)),
            ],
            out_specs=[pl.BlockSpec((QUAD, 1, QKV_ROWS, DB), lambda i, p: (0, i, 0, 0))]
            + [pl.BlockSpec((1, QKV_ROWS, DB), lambda i, p: (i, 0, 0))] * QUAD,
            scratch_shapes=[pltpu.VMEM((D, length), BF16), pltpu.VMEM((QKV, D), F32)],
        ),
        compiler_params=params(),
        name="qkv_grads",
        cost_estimate=pl.CostEstimate(flops=300000000, bytes_accessed=1000000, transcendentals=0),
    )(idx, z, n1t, gg)


CORE = [(i, i ^ 1) for i in range(8)]
ALONG_X = [(i, i ^ 2) for i in range(8)]
ALONG_Y = [(i, i ^ 4) for i in range(8)]
ACROSS = [(i, i ^ 6) for i in range(8)]


def swap(values):
    return lax.ppermute(values, "fsdp", CORE)


def from_z(values, k):
    return lax.ppermute(values, "dp", [(j, (j - k) % QUAD) for j in range(QUAD)])


def to_z(values, k):
    return lax.ppermute(values, "dp", [(j, (j + k) % QUAD) for j in range(QUAD)])


def spread_z(piece):
    return (piece,) + tuple(from_z(piece, k) for k in range(1, QUAD))


def spread_sides(own):
    return (own, lax.ppermute(own, "fsdp", ALONG_X), lax.ppermute(own, "fsdp", ALONG_Y))


def spread_across(own, by_x, by_y):
    return (lax.ppermute(by_y[:2], "fsdp", ALONG_X), lax.ppermute(by_x[2:], "fsdp", ALONG_Y))


def spread_core(pieces):
    return tuple(swap(piece) for piece in pieces)


def add(parts):
    return functools.reduce(jnp.add, [part.astype(F32) for part in parts])


def swap_plane(blocks):
    return (
        blocks[0],
        lax.ppermute(blocks[1], "fsdp", ALONG_X),
        lax.ppermute(blocks[2], "fsdp", ALONG_Y),
        lax.ppermute(blocks[3], "fsdp", ACROSS),
    )


def swap_corner(block):
    half = block.shape[0] // 2
    return (lax.ppermute(block[:half], "fsdp", ALONG_X), lax.ppermute(block[half:], "fsdp", ALONG_Y))


def swap_sides(blocks, corner):
    half = blocks[1].shape[0] // 2
    to_x = jnp.concatenate([blocks[1][:half], add([blocks[1][half:], corner[1]]).astype(BF16)], axis=0)
    to_y = jnp.concatenate([add([blocks[2][:half], corner[0]]).astype(BF16), blocks[2][half:]], axis=0)
    return (blocks[0], lax.ppermute(to_x, "fsdp", ALONG_X), lax.ppermute(to_y, "fsdp", ALONG_Y))


def swap_z(blocks):
    return (blocks[0],) + tuple(to_z(blocks[k], k) for k in range(1, QUAD))


def slab(values, start, size, axis):
    return lax.dynamic_slice_in_dim(values, start, size, axis)


def tables(yx, z, core, first):
    entries = [yx ^ k for k in range(QUAD)] + [(z + k) % QUAD for k in range(QUAD)]
    entries += [core, first, 1 - core, 0, 0, 0, 0, 0]
    return jnp.stack([jnp.asarray(e, jnp.int32) for e in entries])


def gather_near(core, early, gain_attn, w_query, w_key, w_value, w_out, gain_mlp, w_gate, w_up, w_down):
    zero = core == 0
    rows = jnp.concatenate([w_out, w_query, w_key, w_value], axis=1)
    share = rows.shape[0]
    extra = ROWS - share
    pad = jnp.zeros((1, 256 - DB), BF16)
    gains = jnp.concatenate(
        [gain_attn[None], jnp.zeros((1, 256 - share), BF16), gain_mlp[None], jnp.zeros((1, FB - 256 - share), BF16)], axis=1
    )
    sent = jnp.concatenate([rows[0:extra], gains, jnp.zeros((SPARE - extra - 1, FB), BF16)], axis=0)
    taken = swap(sent)
    theirs = taken[extra : extra + 1]
    line = jnp.concatenate(
        [theirs[:, 0:share], gain_attn[None], pad, theirs[:, 256 : 256 + share], gain_mlp[None], jnp.zeros((1, FB - 256 - DB), BF16)],
        axis=1,
    )
    attn = jnp.where(
        zero,
        jnp.concatenate([rows, taken[0:extra]], axis=0),
        jnp.concatenate([jnp.broadcast_to(line, (SPARE, FB)), rows[extra:]], axis=0),
    )
    turned = w_down.T
    taken = swap(slab(turned, (1 - core) * (DB - ROWS), ROWS, 0))
    kept = slab(turned, core * (DB - ROWS), ROWS, 0)
    down = jnp.where(zero, jnp.concatenate([kept, taken], axis=1), jnp.concatenate([taken, kept], axis=1))
    taken = swap(jnp.where(zero, w_up, w_gate))
    pair = jnp.where(zero, jnp.concatenate([w_gate, taken], axis=0), jnp.concatenate([taken, w_up], axis=0))
    pair = spread_z(pair)
    attn = jnp.stack(spread_z(attn) + (down,))
    attn, early = lax.optimization_barrier((attn, early))
    sides = spread_sides(attn)
    return sides + spread_across(*sides), pair, early


def after(values, *others):
    return lax.optimization_barrier((values, others))[0]


def in_pieces(blocks):
    return (blocks[0], blocks[1], blocks[2], blocks[3, 0:2], blocks[3, 2:4])


def gather_any(gain_attn, w_query, w_key, w_value, w_out, gain_mlp, w_gate, w_up, w_down):
    def whole(weight):
        return lax.all_gather(lax.all_gather(weight, "dp", axis=1, tiled=True), "fsdp", axis=0, tiled=True)

    def blocks(weight):
        return weight.reshape(QUAD, weight.shape[0] // QUAD, QUAD, weight.shape[1] // QUAD).transpose(0, 2, 1, 3)

    attn = jnp.concatenate([blocks(whole(w)) for w in (w_out, w_query, w_key, w_value)], axis=3)
    gains = [lax.all_gather(g, "fsdp", axis=0, tiled=True).reshape(QUAD, 1, 1, DB) for g in (gain_attn, gain_mlp)]
    line = jnp.concatenate(
        [gains[0], jnp.zeros((QUAD, 1, 1, 256 - DB), BF16), gains[1], jnp.zeros((QUAD, 1, 1, FB - 256 - DB), BF16)], axis=3
    )
    line = jnp.broadcast_to(line, (QUAD, QUAD, SPARE, FB))
    attn_two = jnp.concatenate([line, attn[:, :, ROWS:]], axis=2)
    down = blocks(whole(w_down).T).transpose(1, 0, 2, 3)
    pair = [in_pieces(blocks(whole(w))) for w in (w_gate, w_up)]
    return (
        in_pieces(attn[:, :, 0:ROWS]) + in_pieces(attn_two),
        pair[0] + pair[1],
        tuple(down[:, z, 0:ROWS] for z in range(QUAD)) + tuple(down[:, z, DB - ROWS :] for z in range(QUAD)),
    )


def on_device(
    near,
    tokens,
    first_len,
    gain_attn,
    w_query,
    w_key,
    w_value,
    w_out,
    gain_mlp,
    w_gate,
    w_up,
    w_down,
    cotangent,
):
    length = tokens.shape[0]
    first = first_len[0]
    weights = (gain_attn, w_query, w_key, w_value, w_out, gain_mlp, w_gate, w_up, w_down)
    if near:
        place = lax.axis_index("fsdp")
        core = place & 1
        idx = tables(place >> 1, lax.axis_index("dp"), core, first)
        attn, pair, (idx, cosine, sine) = gather_near(core, (idx, *rope_tables(first, length)), *weights)
    else:
        core = 0
        idx = tables(0, 0, 0, first)
        attn, pair, down = gather_any(*weights)
        cosine, sine = rope_tables(first, length)
    xt, ct = tokens.T, cotangent.T
    if near:
        down = jnp.stack([attn[0][QUAD], attn[1][QUAD], attn[2][QUAD], attn[4][2]])
        attn = attn + spread_core(attn)
        pair = jnp.stack(pair)
        attn, pair, down = lax.optimization_barrier((attn, pair, down))
        pair = spread_sides(pair)
        down = spread_z(down)
    weight, gains, n1t, qx, kx, kt, vt = call_project(idx, xt, cosine, sine, attn)
    ot, lse = call_attend(qx, kx, vt)
    if near:
        pair, ot = lax.optimization_barrier((pair, ot))
        pair = pair + spread_across(*pair)
    y, n2, n2t = call_leave(xt, gains, weight, ot)
    if near:
        pair, down, n2 = lax.optimization_barrier((pair, down, n2))
        pair = pair + spread_core(pair)
        down = down + spread_core(down)
    mixed, h, dgu, dyt, dat, gain_two = call_feed(idx, n2, y, ct, gains, pair, down)

    halves = gain_two[0].reshape(QUAD, 1, 2, DB // 2)
    row = jnp.pad(halves, ((0, 0), (0, 7), (0, 0), (0, FB // 2 - DB // 2))).reshape(QUAD, 8, FB)
    args_down = (ct, h, ot.reshape(D, length), dat, row)
    pair_theirs = call_pair_grads(idx, n2t, dgu)[0]
    if near:
        came = swap(pair_theirs)
        args_down = after(args_down, pair_theirs)
    else:
        came = jnp.zeros_like(pair_theirs)
    down_theirs = call_down_grads(idx, *args_down)[0]
    if near:
        came_down = swap(down_theirs)
        came = after(came, down_theirs)
    else:
        came_down = jnp.zeros_like(down_theirs)
    pair_mine = call_pair_grads(idx, n2t, dgu, received=came)
    if near:
        pair_corner = swap_corner(pair_mine[3])
        came_down = after(came_down, pair_mine)
    down_mine = call_down_grads(idx, *args_down, received=came_down)
    if near:
        pair_corner, down_mine, dat = lax.optimization_barrier((pair_corner, down_mine, dat))
        pair_got = swap_sides(pair_mine, pair_corner)
        down_corner = swap_corner(down_mine[3])
    do = call_give(weight, dat)
    heads = (qx, kx, kt, vt, ot, do, lse, cosine, sine)
    first_part = call_attend_backward(0, 2, *heads)
    if near:
        heads = after(heads, first_part)
    second_part = call_attend_backward(2, 3, *heads)
    if near:
        pair_got, down_corner, second_part = lax.optimization_barrier((pair_got, down_corner, second_part))
        pair_got = swap_z(add(pair_got).astype(BF16))
        down_got = swap_sides(down_mine, down_corner)
    grad_tokens, turned, gain_one = call_enter_backward(xt, dyt, gains, weight, *first_part, *second_part)
    row = jnp.pad(gain_one[0].reshape(QUAD, 1, DB), ((0, 0), (0, 7), (0, 0)))
    qkv_theirs, *qkv_mine = call_qkv_grads(idx, turned, n1t, row)
    if near:
        pair_got, down_got, qkv_theirs = lax.optimization_barrier((pair_got, down_got, qkv_theirs))
        came = swap(qkv_theirs)
        qkv_got = swap_plane([add([part, came[k]]).astype(BF16) for k, part in enumerate(qkv_mine)])
        down_got = swap_z(add(down_got).astype(BF16))
        pair_sum = add(pair_got)
        qkv_got, down_got, pair_sum = lax.optimization_barrier((qkv_got, down_got, pair_sum))
        qkv_got = swap_z(add(qkv_got).astype(BF16))
        down_sum, qkv_sum = add(down_got), add(qkv_got)
        outs = settle_near(core, down_sum, pair_sum, qkv_sum)
    else:
        outs = settle_any(down_mine, down_theirs, pair_mine, pair_theirs, qkv_mine, qkv_theirs, gain_one[0], gain_two[0])
    return (mixed.T, grad_tokens.T) + outs


def settle_near(core, down_sum, pair_sum, qkv_sum):
    zero = core == 0
    share = DB // 2

    kept = slab(pair_sum, core * share, share, 0)
    taken = swap(slab(pair_sum, (1 - core) * share, share, 0).astype(BF16)).astype(F32)
    grad_gate, grad_up = jnp.where(zero, kept, taken), jnp.where(zero, taken, kept)

    grad_out = jnp.where(zero, down_sum[0:share, FB : FB + DB], down_sum[ROWS - share :, FB : FB + DB])
    half = FB // 2
    kept = slab(down_sum, core * half, half, 1)
    taken = swap(slab(down_sum, (1 - core) * half, half, 1).astype(BF16)).astype(F32)
    upper, lower = jnp.where(zero, kept, taken), jnp.where(zero, taken, kept)
    grad_down = jnp.concatenate([upper, lower[SPARE:]], axis=0).T
    grad_gain_mlp = lower[0, 0:share]

    kept = slab(qkv_sum, core * share, share, 1)
    taken = swap(slab(qkv_sum, (1 - core) * share, share, 1).astype(BF16)).astype(F32)
    upper, lower = jnp.where(zero, kept, taken), jnp.where(zero, taken, kept)
    grad_gain_attn = lower[0]
    rows = jnp.concatenate([upper, lower[SPARE:]], axis=0).T
    return (
        grad_gain_attn, rows[:, 0:QB], rows[:, QB : QB + KB], rows[:, QB + KB :], grad_out,
        grad_gain_mlp, grad_gate, grad_up, grad_down,
    )


def settle_any(down_mine, down_theirs, pair_mine, pair_theirs, qkv_mine, qkv_theirs, gain_one, gain_two):
    def whole(blocks):
        return blocks.transpose(0, 2, 1, 3).reshape(blocks.shape[0] * blocks.shape[2], -1)

    def shard(values):
        values = lax.psum_scatter(values, "fsdp", scatter_dimension=0, tiled=True)
        return lax.psum_scatter(values, "dp", scatter_dimension=1, tiled=True).astype(F32)

    def gain(values):
        values = lax.psum(values, "dp")
        return lax.psum_scatter(values, "fsdp", scatter_dimension=0, tiled=True)

    both = jnp.concatenate([jnp.stack(down_mine), down_theirs[:, :, SPARE:]], axis=2)
    grad_down = shard(whole(both[..., 0:FB].transpose(1, 0, 2, 3)).T)
    grad_out = shard(whole(both[..., FB : FB + DB]))
    grad_gate, grad_up = shard(whole(jnp.stack(pair_mine))), shard(whole(pair_theirs))
    both = jnp.concatenate([jnp.stack(qkv_mine), qkv_theirs[:, :, SPARE:]], axis=2).transpose(0, 1, 3, 2)
    grad_query = shard(whole(both[..., 0:QB]))
    grad_key = shard(whole(both[..., QB : QB + KB]))
    grad_value = shard(whole(both[..., QB + KB :]))
    return (
        gain(gain_one), grad_query, grad_key, grad_value, grad_out, gain(gain_two), grad_gate, grad_up, grad_down,
    )


def solution(mesh):
    sizes = dict(mesh.shape)
    near = sizes["fsdp"] == 8 and sizes["dp"] == QUAD
    in_specs = (
        P(("fsdp", "dp"), None),
        P(("fsdp", "dp")),
        P("fsdp"),
        P("fsdp", "dp"),
        P("fsdp", "dp"),
        P("fsdp", "dp"),
        P("fsdp", "dp"),
        P("fsdp"),
        P("fsdp", "dp"),
        P("fsdp", "dp"),
        P("fsdp", "dp"),
        P(("fsdp", "dp"), None),
    )
    out_specs = (
        P(("fsdp", "dp"), None),
        P(("fsdp", "dp"), None),
        P("fsdp"),
        P("fsdp", "dp"),
        P("fsdp", "dp"),
        P("fsdp", "dp"),
        P("fsdp", "dp"),
        P("fsdp"),
        P("fsdp", "dp"),
        P("fsdp", "dp"),
        P("fsdp", "dp"),
    )
    return jax.shard_map(
        functools.partial(on_device, near), mesh=mesh, in_specs=in_specs, out_specs=out_specs, check_vma=False
    )
```

```python
import functools

import jax
import jax.numpy as jnp
from jax import lax
from jax.experimental import pallas as pl
from jax.experimental.pallas import tpu as pltpu
from jax.sharding import PartitionSpec as P

D = 960
FF = 2560
HEADS = 15
KV_HEADS = 5
GROUP = HEADS // KV_HEADS
HEAD_DIM = 64
HALF = HEAD_DIM // 2
TILE = 256
QUAD = 4
DB = D // QUAD
FB = FF // QUAD
QB = D // QUAD
KB = KV_HEADS * HEAD_DIM // QUAD
ROWS = 128
SPARE = 16
QKV = QB + 2 * KB
QKV_ROWS = 208
LEAD = FB - 512
SKIP = DB - LEAD
NEG = -1e30
EPS = 1e-05
ROPE_BASE = 10000.0
BIG = 60 * 1024 * 1024

F32 = jnp.float32
BF16 = jnp.bfloat16


def nn(a, b):
    return jnp.dot(a, b, preferred_element_type=F32)


def nt(a, b):
    return lax.dot_general(a, b, (((1,), (1,)), ((), ())), preferred_element_type=F32)


def rope_tables(first, length):
    places = jnp.arange(length, dtype=jnp.int32)
    position = jnp.where(places < first, places, places - first).astype(F32)
    frequency = ROPE_BASE ** (-jnp.arange(0, HEAD_DIM, 2, dtype=F32) / HEAD_DIM)
    angles = frequency[:, None] * position[None, :]
    return jnp.cos(angles), jnp.sin(angles)


def params():
    return pltpu.CompilerParams(vmem_limit_bytes=BIG)


def any_spec():
    return pl.BlockSpec(memory_space=pl.ANY)


def by_plane_halved(pieces, k, kz):
    if k < 3:
        return pieces[k].at[kz]
    return pieces[3 + kz // 2].at[kz % 2]


def by_z(pieces, k, kz):
    return pieces[kz].at[k]


def copies(idx, pieces, pick, sems, target):
    plans = ([], [])
    mine, other = pieces[: len(pieces) // 2], pieces[len(pieces) // 2 :]
    for mine_core in range(2):
        slot = 0
        for core, found in ((mine_core, mine), (1 - mine_core, other)):
            for k in range(QUAD):
                for kz in range(QUAD):
                    ref = pick(found, k, kz)
                    for source, dest in target(core, idx[4 + kz], idx[k], kz):
                        src = ref if source is None else ref.at[pl.ds(*source), :]
                        plans[mine_core].append(
                            pltpu.make_async_copy(src, dest, sems.at[slot])
                        )
                        slot += 1
    return plans


def rows_target(weight, gains=None):
    def target(core, z, yx, kz):
        base = pl.multiple_of(yx * DB, 16)
        if core == 0:
            return [((0, ROWS), weight.at[z, pl.ds(base, ROWS), :])]
        found = [((SPARE, DB - ROWS), weight.at[z, pl.ds(base + ROWS, DB - ROWS), :])]
        if gains is not None and kz == 0:
            found.append(((0, SPARE), gains.at[yx]))
        return found

    return target


def down_target(weight):
    def target(core, z, yx, kz):
        base = pl.multiple_of(z * DB, 16)
        columns = pl.ds(pl.multiple_of(yx * FB, 128), FB)
        if core == 0:
            return [((0, ROWS), weight.at[pl.ds(base, ROWS), columns])]
        return [((SPARE, DB - ROWS), weight.at[pl.ds(base + ROWS, DB - ROWS), columns])]

    return target


def pair_target(weight):
    def target(core, z, yx, kz):
        base = pl.multiple_of(yx * DB, 16)
        columns = pl.ds(pl.multiple_of(z * FB, 128), FB)
        return [(None, weight.at[core, pl.ds(base, DB), columns])]

    return target


def run_copies(core, plans):
    for c in range(2):

        @pl.when(core == c)
        def _():
            for copy in plans[c]:
                copy.start()
            for copy in plans[c]:
                copy.wait()


def norm_columns(x, axis):
    return lax.rsqrt(jnp.mean(x * x, axis=axis, keepdims=True) + EPS)


def column(row):
    return jnp.broadcast_to(row, (128, row.shape[1])).T[:, 0:1]


def project(idx, xt_ref, cos_ref, sin_ref, *rest):
    weight, gain_ref, n1t_ref, qx_ref, kx_ref, kt_ref, vt_ref, gains, sems = rest[10:]
    run_copies(idx[8], copies(idx, rest[0:10], by_plane_halved, sems, rows_target(weight, gains)))
    length = xt_ref.shape[1]
    first = idx[9]
    gain_one = jnp.concatenate([gains[b, 0:1, 0:DB] for b in range(QUAD)], axis=1).astype(F32)
    gain_two = jnp.concatenate([gains[b, 0:1, 256 : 256 + DB] for b in range(QUAD)], axis=1).astype(F32)
    gain_ref[0:1, :] = gain_one
    gain_ref[1:2, :] = gain_two
    gain_column = column(gain_one)

    place = lax.broadcasted_iota(jnp.int32, (HEAD_DIM, length), 1)
    row = lax.broadcasted_iota(jnp.int32, (HEAD_DIM, length), 0)
    extra_q = jnp.where((row == 0) & (place >= first), NEG, 0.0).astype(BF16)
    extra_k = jnp.where((row == 0) & (place < first), 1.0, 0.0)
    for h in range(HEADS):
        qx_ref[h, HEAD_DIM:, :] = extra_q

    def tile(i, carry):
        at = pl.ds(pl.multiple_of(i * FEED_TILE, FEED_TILE), FEED_TILE)
        x = xt_ref[:, at].astype(F32)
        n1t = (x * norm_columns(x, 0) * gain_column).astype(BF16)
        n1t_ref[:, at] = n1t
        n1 = n1t.T
        cosine, sine = cos_ref[:, at], sin_ref[:, at]
        flat = [nn(n1, weight[z, :, LEAD:]).T for z in range(QUAD)]
        queries = jnp.concatenate([f[SKIP : SKIP + QB] for f in flat], axis=0)
        keys = jnp.concatenate([f[SKIP + QB : SKIP + QB + KB] for f in flat], axis=0)
        values = jnp.concatenate([f[SKIP + QB + KB :] for f in flat], axis=0)

        def turn(u):
            u1, u2 = u[:HALF], u[HALF:]
            return jnp.concatenate([u1 * cosine - u2 * sine, u2 * cosine + u1 * sine], axis=0).astype(BF16)

        for h in range(HEADS):
            qx_ref[h, 0:HEAD_DIM, at] = turn(queries[h * HEAD_DIM : (h + 1) * HEAD_DIM]) * jnp.asarray(0.125, BF16)
        for h in range(KV_HEADS):
            kt_ref[h, :, at] = turn(keys[h * HEAD_DIM : (h + 1) * HEAD_DIM])
        vt_ref[:, :, at] = values.astype(BF16).reshape(KV_HEADS, HEAD_DIM, FEED_TILE)
        return carry

    lax.fori_loop(0, length // FEED_TILE, tile, 0)
    for j in range(KV_HEADS):
        wide = jnp.concatenate([kt_ref[j].astype(F32), extra_k], axis=0)
        kx_ref[j] = wide.T.astype(BF16)


def call_project(idx, xt, cosine, sine, pieces):
    length = xt.shape[1]
    s = jax.ShapeDtypeStruct
    vm = pl.BlockSpec(memory_space=pltpu.VMEM)
    return pl.pallas_call(
        project,
        out_shape=(
            s((QUAD, D, FB), BF16),
            s((8, D), F32),
            s((D, length), BF16),
            s((HEADS, 2 * HEAD_DIM, length), BF16),
            s((KV_HEADS, length, 2 * HEAD_DIM), BF16),
            s((KV_HEADS, HEAD_DIM, length), BF16),
            s((KV_HEADS, HEAD_DIM, length), BF16),
        ),
        in_specs=[pl.BlockSpec(memory_space=pltpu.SMEM)] + [vm] * 3 + [any_spec()] * 10,
        out_specs=(vm,) * 7,
        scratch_shapes=[
            pltpu.VMEM((QUAD, SPARE, FB), BF16),
            pltpu.SemaphoreType.DMA((64,)),
        ],
        compiler_params=params(),
        name="project",
        cost_estimate=pl.CostEstimate(flops=600000000, bytes_accessed=2000000, transcendentals=0),
    )(idx, xt, cosine, sine, *pieces)


def causal_mask():
    return lax.broadcasted_iota(jnp.int32, (TILE, GROUP * TILE), 0) > (
        lax.broadcasted_iota(jnp.int32, (TILE, GROUP * TILE), 1) % TILE
    )


def attend(qx_ref, kx_ref, vt_ref, ot_ref, lse_ref, raw_s, p_s):
    tiles = qx_ref.shape[2] // TILE
    causal = causal_mask()
    for b in range(tiles):
        at = slice(b * TILE, (b + 1) * TILE)
        span = (b + 1) * TILE
        qx = jnp.concatenate([qx_ref[g, :, at] for g in range(GROUP)], axis=1)
        raw_s[0:span, :] = nn(kx_ref[0, 0:span, :], qx)
        raw_s[at, :] = jnp.where(causal, NEG, raw_s[at, :])
        highest = jnp.max(raw_s[0:span, :], axis=0, keepdims=True)
        total = 0.0
        for s in range(b + 1):
            keys = slice(s * TILE, (s + 1) * TILE)
            weights = jnp.exp(raw_s[keys, :] - highest)
            total = total + jnp.sum(weights, axis=0, keepdims=True)
            p_s[keys, :] = weights.astype(BF16)
        out = nn(vt_ref[0, :, 0:span], p_s[0:span, :]) / total
        lse_ref[0, b] = highest + jnp.log(total)
        for g in range(GROUP):
            ot_ref[g, :, at] = out[:, g * TILE : (g + 1) * TILE].astype(BF16)


def heads_spec(count, rows, length):
    return pl.BlockSpec((count, rows, length), lambda j: (j, 0, 0))


def call_attend(qx, kx, vt):
    length = qx.shape[2]
    tiles = length // TILE
    s = jax.ShapeDtypeStruct
    return pl.pallas_call(
        attend,
        out_shape=(
            s((HEADS, HEAD_DIM, length), BF16),
            s((KV_HEADS, tiles, 1, GROUP * TILE), F32),
        ),
        grid=(KV_HEADS,),
        in_specs=[
            heads_spec(GROUP, 2 * HEAD_DIM, length),
            heads_spec(1, length, 2 * HEAD_DIM),
            heads_spec(1, HEAD_DIM, length),
        ],
        out_specs=[
            heads_spec(GROUP, HEAD_DIM, length),
            pl.BlockSpec((1, tiles, 1, GROUP * TILE), lambda j: (j, 0, 0, 0)),
        ],
        scratch_shapes=[
            pltpu.VMEM((length, GROUP * TILE), F32),
            pltpu.VMEM((length, GROUP * TILE), BF16),
        ],
        compiler_params=params(),
        name="attend",
        cost_estimate=pl.CostEstimate(flops=2000000000, bytes_accessed=800000, transcendentals=0),
    )(qx, kx, vt)


def leave(xt_ref, gain_ref, weight, ot_ref, y_ref, n2_ref, n2t_ref):
    o = ot_ref[...].reshape(D, ot_ref.shape[2]).T
    added = jnp.concatenate([nn(o, weight[z])[:, 0:DB] for z in range(QUAD)], axis=1)
    y = xt_ref[...].T.astype(F32) + added
    y_ref[...] = y
    n2 = (y * norm_columns(y, -1) * gain_ref[1:2, :]).astype(BF16)
    n2_ref[...] = n2
    n2t_ref[...] = n2.T


def call_leave(xt, gains, weight, ot):
    length = xt.shape[1]
    s = jax.ShapeDtypeStruct
    tall = pl.BlockSpec((D, FEED_TILE), lambda i: (0, i))
    wide = pl.BlockSpec((FEED_TILE, D), lambda i: (i, 0))
    return pl.pallas_call(
        leave,
        out_shape=(s((length, D), F32), s((length, D), BF16), s((D, length), BF16)),
        grid=(length // FEED_TILE,),
        in_specs=[
            tall,
            pl.BlockSpec((8, D), lambda i: (0, 0)),
            pl.BlockSpec((QUAD, D, 256), lambda i: (0, 0, 0)),
            pl.BlockSpec((HEADS, HEAD_DIM, FEED_TILE), lambda i: (0, 0, i)),
        ],
        out_specs=[wide, wide, tall],
        compiler_params=params(),
        name="leave",
        cost_estimate=pl.CostEstimate(flops=300000000, bytes_accessed=1500000, transcendentals=0),
    )(xt, gains, weight, ot)


def feed(idx, n2_ref, y_ref, ct_ref, gain_ref, *rest):
    pairs, downs = rest[0:10], rest[10:18]
    mixed_ref, h_ref, dgu_ref, dyt_ref, dat_ref, gg_ref, weight, down, sems = rest[18:]

    @pl.when(pl.program_id(0) == 0)
    def _():
        first = copies(idx, pairs, by_plane_halved, sems.at[0], pair_target(weight))
        second = copies(idx, downs, by_z, sems.at[1], down_target(down))
        run_copies(idx[8], [a + b for a, b in zip(first, second)])
        gg_ref[...] = jnp.zeros_like(gg_ref)

    n2 = n2_ref[...]
    chunks = [slice(b, b + FEED_CHUNK) for b in range(0, FF, FEED_CHUNK)]
    for at in chunks:
        g = nn(n2, weight[0, :, at])
        u = nn(n2, weight[1, :, at])
        sig = 1.0 / (1.0 + jnp.exp(-g))
        silu = g * sig
        h_ref[:, at] = (silu * u).astype(BF16)
        dgu_ref[0, :, at] = (u * (sig + silu * (1.0 - sig))).astype(BF16)
        dgu_ref[1, :, at] = silu.astype(BF16)
    y = y_ref[...]
    mixed_ref[...] = (y + nt(h_ref[...], down[...])).astype(BF16).T
    c = ct_ref[...].T
    for at in chunks:
        dh = nn(c, down[:, at])
        dgu_ref[0, :, at] = (dh * dgu_ref[0, :, at].astype(F32)).astype(BF16)
        dgu_ref[1, :, at] = (dh * dgu_ref[1, :, at].astype(F32)).astype(BF16)
    dn2 = nt(dgu_ref[0], weight[0]) + nt(dgu_ref[1], weight[1])
    r = norm_columns(y, -1)
    yr = y * r
    gg_ref[0:1, :] += jnp.sum(dn2 * yr, axis=0, keepdims=True)
    t = dn2 * gain_ref[1:2, :]
    dy = c.astype(F32) + r * (t - yr * jnp.mean(t * yr, axis=-1, keepdims=True))
    dyt = dy.T
    dyt_ref[...] = dyt
    dat_ref[...] = dyt.astype(BF16)


FEED_TILE = 512
FEED_CHUNK = 512


def call_feed(idx, n2, y, ct, gains, pairs, downs):
    length = n2.shape[0]
    s = jax.ShapeDtypeStruct
    wide = pl.BlockSpec((FEED_TILE, D), lambda i, p: (i, 0))
    tall = pl.BlockSpec((D, FEED_TILE), lambda i, p: (0, i))
    whole = pl.BlockSpec((8, D), lambda i, p: (0, 0))
    return pl.pallas_call(
        feed,
        out_shape=(
            s((D, length), BF16),
            s((length, FF), BF16),
            s((2, length, FF), BF16),
            s((D, length), F32),
            s((D, length), BF16),
            s((8, D), F32),
        ),
        grid_spec=pltpu.PrefetchScalarGridSpec(
            num_scalar_prefetch=1,
            grid=(length // FEED_TILE,),
            in_specs=[wide, wide, tall, whole] + [any_spec()] * 18,
            out_specs=[
                tall,
                pl.BlockSpec((FEED_TILE, FF), lambda i, p: (i, 0)),
                pl.BlockSpec((2, FEED_TILE, FF), lambda i, p: (0, i, 0)),
                tall,
                tall,
                whole,
            ],
            scratch_shapes=[
                pltpu.VMEM((2, D, FF), BF16),
                pltpu.VMEM((D, FF), BF16),
                pltpu.SemaphoreType.DMA((2, 64)),
            ],
        ),
        compiler_params=params(),
        name="feed_forward_backward",
        cost_estimate=pl.CostEstimate(flops=3000000000, bytes_accessed=5000000, transcendentals=0),
    )(idx, n2, y, ct, gains, *pairs, *downs)


def pair_grads(target, idx, n2t_ref, d_ref, *rest):
    full = rest[-1]
    received, outs = (rest[0:1], rest[1:-1]) if target == 0 else ((), rest[:-1])
    full[...] = nn(n2t_ref[...], d_ref[...])
    for k in range(QUAD):
        got = full[pl.ds(pl.multiple_of(idx[k] * DB, 16), DB), :]
        if received:
            got = got + received[0][k, 0].astype(F32)
        if len(outs) == 1:
            outs[0][k, 0] = got.astype(BF16)
        else:
            outs[k][0] = got.astype(BF16)


def call_pair_grads(idx, n2t, dgu, received=None):
    length = n2t.shape[1]
    s = jax.ShapeDtypeStruct
    block = pl.BlockSpec((QUAD, 1, DB, FB), lambda i, p: (0, i, 0, 0))
    matrix = 10 if received is None else 8
    specs = [
        pl.BlockSpec((D, length), lambda i, p: (0, 0)),
        pl.BlockSpec((None, length, FB), lambda i, p: (p[matrix], 0, p[4 + i])),
    ]
    if received is None:
        out_shape = [s((QUAD, QUAD, DB, FB), BF16)]
        out_specs = [block]
        extra = ()
    else:
        specs.append(block)
        extra = (received,)
        out_shape = [s((QUAD, DB, FB), BF16)] * QUAD
        out_specs = [pl.BlockSpec((1, DB, FB), lambda i, p: (i, 0, 0))] * QUAD
    return pl.pallas_call(
        functools.partial(pair_grads, 1 if received is None else 0),
        out_shape=out_shape,
        grid_spec=pltpu.PrefetchScalarGridSpec(
            num_scalar_prefetch=1,
            grid=(QUAD,),
            in_specs=specs,
            out_specs=out_specs,
            scratch_shapes=[pltpu.VMEM((D, FB), F32)],
        ),
        compiler_params=params(),
        name="pair_grads",
        cost_estimate=pl.CostEstimate(flops=500000000, bytes_accessed=1500000, transcendentals=0),
    )(idx, n2t, dgu, *extra)


WIDE = FB + 256


def down_grads(which, idx, ct_ref, h_ref, ot_ref, dat_ref, gg_ref, *rest):
    right, also = rest[-2:]
    received, outs = (rest[0:1], rest[1:-2]) if which == 8 else ((), rest[:-2])
    core = idx[which]
    k = pl.program_id(0)
    yx = idx[k]
    offset = core * (DB - ROWS)

    def rows(ref, block, size, shift):
        return ref[pl.ds(pl.multiple_of(block * DB + shift, 16), size), :]

    @pl.when(k == 0)
    def _():
        for kz in range(QUAD):
            right[kz * DB : (kz + 1) * DB, :] = rows(dat_ref, idx[4 + kz], DB, 0)
        left = jnp.concatenate([rows(ot_ref, idx[i], ROWS, offset) for i in range(QUAD)], axis=0)
        also[...] = nt(left, right[...]).reshape(QUAD, ROWS, D)

    left = jnp.concatenate([rows(ct_ref, idx[4 + kz], ROWS, offset) for kz in range(QUAD)], axis=0)
    full = nn(left, h_ref[...])
    spare = jnp.broadcast_to(gg_ref[yx, 0:1, :], (SPARE, FB))

    def put(ref, kz):
        got = full[kz * ROWS : (kz + 1) * ROWS]
        out = also[k, :, kz * DB : (kz + 1) * DB]
        head = jnp.where(core == 1, spare, got[0:SPARE])
        if received:
            got = got + received[0][0, kz, :, 0:FB].astype(F32)
            out = out + received[0][0, kz, :, FB : FB + DB].astype(F32)
            head = head + received[0][0, kz, 0:SPARE, 0:FB].astype(F32)
        ref[:, 0:FB] = got.astype(BF16)
        ref[:, FB : FB + DB] = out.astype(BF16)
        ref[:, FB + DB :] = jnp.zeros((ROWS, 256 - DB), BF16)
        ref[0:SPARE, 0:FB] = head.astype(BF16)

    if len(outs) == 1:
        for kz in range(QUAD):
            put(outs[0].at[0, kz], kz)
    else:
        for i in range(QUAD):

            @pl.when(k == i)
            def _():
                for kz in range(QUAD):
                    put(outs[i].at[kz], kz)


def call_down_grads(idx, ct, h, ot, dat, gg, received=None):
    length = ct.shape[1]
    s = jax.ShapeDtypeStruct
    block = pl.BlockSpec((1, QUAD, ROWS, WIDE), lambda i, p: (i, 0, 0, 0))
    vm = pl.BlockSpec((D, length), lambda i, p: (0, 0))
    specs = [
        vm,
        pl.BlockSpec((length, FB), lambda i, p: (0, p[i])),
        vm,
        vm,
        pl.BlockSpec((QUAD, 8, FB), lambda i, p: (0, 0, 0)),
    ]
    if received is None:
        out_shape, out_specs, extra = [s((QUAD, QUAD, ROWS, WIDE), BF16)], [block], ()
    else:
        specs.append(block)
        extra = (received,)
        out_shape = [s((QUAD, ROWS, WIDE), BF16)] * QUAD
        out_specs = [pl.BlockSpec((QUAD, ROWS, WIDE), lambda i, p: (0, 0, 0))] * QUAD
    return pl.pallas_call(
        functools.partial(down_grads, 10 if received is None else 8),
        out_shape=out_shape,
        grid_spec=pltpu.PrefetchScalarGridSpec(
            num_scalar_prefetch=1,
            grid=(QUAD,),
            in_specs=specs,
            out_specs=out_specs,
            scratch_shapes=[pltpu.VMEM((D, length), BF16), pltpu.VMEM((QUAD, ROWS, D), F32)],
        ),
        compiler_params=params(),
        name="down_grads",
        cost_estimate=pl.CostEstimate(flops=400000000, bytes_accessed=1500000, transcendentals=0),
    )(idx, ct, h, ot, dat, gg, *extra)


def give(weight, dat_ref, do_ref):
    total = 0.0
    for z in range(QUAD):
        total = total + nn(weight[z, :, 0:DB], dat_ref[z * DB : (z + 1) * DB, :])
    do_ref[...] = total.astype(BF16).reshape(do_ref.shape)


def call_give(weight, dat):
    length = dat.shape[1]
    return pl.pallas_call(
        give,
        out_shape=jax.ShapeDtypeStruct((HEADS, HEAD_DIM, length), BF16),
        grid=(length // FEED_TILE,),
        in_specs=[
            pl.BlockSpec((QUAD, D, 256), lambda i: (0, 0, 0)),
            pl.BlockSpec((D, FEED_TILE), lambda i: (0, i)),
        ],
        out_specs=pl.BlockSpec((HEADS, HEAD_DIM, FEED_TILE), lambda i: (0, 0, i)),
        compiler_params=params(),
        name="give",
        cost_estimate=pl.CostEstimate(flops=200000000, bytes_accessed=600000, transcendentals=0),
    )(weight, dat)


def unrotate(grads, cosine, sine):
    u1, u2 = grads[:HALF], grads[HALF:]
    return jnp.concatenate([u1 * cosine + u2 * sine, u2 * cosine - u1 * sine], axis=0)


def attend_backward(
    qx_ref, kx_ref, kt_ref, vt_ref, ot_ref, do_ref, lse_ref, cos_ref, sin_ref, zq, zk, zv,
    dk_s, dv_s, raw_s, dp_s, p_s, ds_s,
):
    tiles = qx_ref.shape[2] // TILE
    causal = causal_mask()
    values = vt_ref[0].astype(F32).T.astype(BF16)
    for b in reversed(range(tiles)):
        at = slice(b * TILE, (b + 1) * TILE)
        span = (b + 1) * TILE
        qx = jnp.concatenate([qx_ref[g, :, at] for g in range(GROUP)], axis=1)
        do = jnp.concatenate([do_ref[g, :, at] for g in range(GROUP)], axis=1)
        o = jnp.concatenate([ot_ref[g, :, at] for g in range(GROUP)], axis=1)
        inner = jnp.sum(do.astype(F32) * o.astype(F32), axis=0, keepdims=True)
        log_total = lse_ref[0, b]
        raw_s[0:span, :] = nn(kx_ref[0, 0:span, :], qx)
        dp_s[0:span, :] = nn(values[0:span, :], do)
        for s in range(b + 1):
            keys = slice(s * TILE, (s + 1) * TILE)
            raw = raw_s[keys, :]
            if s == b:
                raw = jnp.where(causal, NEG, raw)
            probs = jnp.exp(raw - log_total)
            p_s[keys, :] = probs.astype(BF16)
            ds_s[keys, :] = (probs * (dp_s[keys, :] - inner)).astype(BF16)
        dq = nn(kt_ref[0, :, 0:span], ds_s[0:span, :])
        dk = nt(ds_s[0:span, :], qx[0:HEAD_DIM, :])
        dv = nt(p_s[0:span, :], do)
        if b == tiles - 1:
            dk_s[...] = dk
            dv_s[...] = dv
        else:
            dk_s[0:span, :] += dk
            dv_s[0:span, :] += dv
        cosine, sine = cos_ref[:, at], sin_ref[:, at]
        for g in range(GROUP):
            part = unrotate(dq[:, g * TILE : (g + 1) * TILE] * 0.125, cosine, sine)
            zq[g, :, at] = part.astype(BF16)
    zk[0] = unrotate(dk_s[...].T, cos_ref[...], sin_ref[...]).astype(BF16)
    zv[0] = dv_s[...].T.astype(BF16)


def call_attend_backward(start, count, qx, kx, kt, vt, ot, do, lse, cosine, sine):
    length = qx.shape[2]
    tiles = length // TILE
    s = jax.ShapeDtypeStruct

    def spec(heads, rows, lanes):
        return pl.BlockSpec((heads, rows, lanes), lambda j: (j + start, 0, 0))

    table = pl.BlockSpec((HALF, length), lambda j: (0, 0))
    return pl.pallas_call(
        attend_backward,
        out_shape=(
            s((GROUP * count, HEAD_DIM, length), BF16),
            s((count, HEAD_DIM, length), BF16),
            s((count, HEAD_DIM, length), BF16),
        ),
        grid=(count,),
        in_specs=[
            spec(GROUP, 2 * HEAD_DIM, length),
            spec(1, length, 2 * HEAD_DIM),
            spec(1, HEAD_DIM, length),
            spec(1, HEAD_DIM, length),
            spec(GROUP, HEAD_DIM, length),
            spec(GROUP, HEAD_DIM, length),
            pl.BlockSpec((1, tiles, 1, GROUP * TILE), lambda j: (j + start, 0, 0, 0)),
            table,
            table,
        ],
        out_specs=[
            heads_spec(GROUP, HEAD_DIM, length),
            heads_spec(1, HEAD_DIM, length),
            heads_spec(1, HEAD_DIM, length),
        ],
        scratch_shapes=[
            pltpu.VMEM((length, HEAD_DIM), F32),
            pltpu.VMEM((length, HEAD_DIM), F32),
            pltpu.VMEM((length, GROUP * TILE), F32),
            pltpu.VMEM((length, GROUP * TILE), F32),
            pltpu.VMEM((length, GROUP * TILE), BF16),
            pltpu.VMEM((length, GROUP * TILE), BF16),
        ],
        compiler_params=params(),
        name="attend_backward",
        cost_estimate=pl.CostEstimate(flops=1000000000, bytes_accessed=1000000, transcendentals=0),
    )(qx, kx, kt, vt, ot, do, lse, cosine, sine)


def enter_backward(idx, xt_ref, dyt_ref, gain_ref, weight, *rest):
    parts, (gx_ref, gg_ref, sums) = rest[:-3], rest[-3:]
    i = pl.program_id(0)

    @pl.when(i == 0)
    def _():
        sums[...] = jnp.zeros_like(sums)

    def flat(found):
        return jnp.concatenate([ref[...].reshape(-1, TILE) for ref in found], axis=0)

    zq, zk, zv = flat(parts[0::3]), flat(parts[1::3]), flat(parts[2::3])
    dn1 = 0.0
    for z in range(QUAD):
        block = jnp.concatenate(
            [
                jnp.zeros((SKIP, TILE), BF16),
                zq[z * QB : (z + 1) * QB],
                zk[z * KB : (z + 1) * KB],
                zv[z * KB : (z + 1) * KB],
            ],
            axis=0,
        )
        dn1 = dn1 + nn(weight[z, :, LEAD:], block)
    x = xt_ref[...].astype(F32)
    r = norm_columns(x, 0)
    xr = x * r
    found = dn1 * xr
    sums[...] += found[:, 0:128] + found[:, 128:256]
    t = dn1 * column(gain_ref[0:1, :])
    gx = dyt_ref[...] + r * (t - xr * jnp.mean(t * xr, axis=0, keepdims=True))
    gx_ref[...] = gx.astype(BF16)

    @pl.when(i == pl.num_programs(0) - 1)
    def _():
        for k in range(QUAD):
            rows = sums[pl.ds(pl.multiple_of(idx[k] * DB, 16), DB), :]
            gg_ref[k] = jnp.broadcast_to(jnp.sum(rows.T, axis=0, keepdims=True), (8, DB))


def call_enter_backward(idx, xt, dyt, gains, weight, *parts):
    length = xt.shape[1]
    s = jax.ShapeDtypeStruct
    tall = pl.BlockSpec((D, TILE), lambda i, p: (0, i))
    return pl.pallas_call(
        enter_backward,
        out_shape=(s((D, length), BF16), s((QUAD, 8, DB), F32)),
        grid_spec=pltpu.PrefetchScalarGridSpec(
            num_scalar_prefetch=1,
            grid=(length // TILE,),
            in_specs=[
                tall,
                tall,
                pl.BlockSpec((8, D), lambda i, p: (0, 0)),
                pl.BlockSpec((QUAD, D, FB), lambda i, p: (0, 0, 0)),
            ]
            + [pl.BlockSpec((part.shape[0], HEAD_DIM, TILE), lambda i, p: (0, 0, i)) for part in parts],
            out_specs=[tall, pl.BlockSpec((QUAD, 8, DB), lambda i, p: (0, 0, 0))],
            scratch_shapes=[pltpu.VMEM((D, 128), F32)],
        ),
        compiler_params=params(),
        name="enter_backward",
        cost_estimate=pl.CostEstimate(flops=400000000, bytes_accessed=1500000, transcendentals=0),
    )(idx, xt, dyt, gains, weight, *parts)


def qkv_grads(idx, n1t_ref, gg_ref, *rest):
    parts, (theirs, *mine), (flat, right, full) = rest[0:6], rest[6:-3], rest[-3:]

    @pl.when(pl.program_id(0) == 0)
    def _():
        at = 0
        for found in (parts[0::3], parts[1::3], parts[2::3]):
            for ref in found:
                rows = ref[...].reshape(-1, ref.shape[2])
                flat[at : at + rows.shape[0], :] = rows
                at += rows.shape[0]
        for k in range(QUAD):
            right[k * DB : (k + 1) * DB, :] = n1t_ref[pl.ds(pl.multiple_of(idx[k] * DB, 16), DB), :]

    z = idx[4 + pl.program_id(0)]
    width = KV_HEADS * HEAD_DIM
    left = jnp.concatenate(
        [
            flat[pl.ds(pl.multiple_of(z * QB, 16), QB), :],
            flat[pl.ds(pl.multiple_of(D + z * KB, 16), KB), :],
            flat[pl.ds(pl.multiple_of(D + width + z * KB, 16), KB), :],
        ],
        axis=0,
    )
    full[...] = nt(left, right[...])
    for which in (10, 8):
        part = full[pl.ds(pl.multiple_of(idx[which] * (QKV - QKV_ROWS), 16), QKV_ROWS), :]
        for k in range(QUAD):
            got = part[:, k * DB : (k + 1) * DB]
            spare = jnp.broadcast_to(gg_ref[k, 0:1, :], (SPARE, DB))
            ref = theirs.at[k, 0] if which == 10 else mine[k].at[0]
            ref[...] = got.astype(BF16)
            ref[0:SPARE, :] = jnp.where(idx[which] == 1, spare, got[0:SPARE]).astype(BF16)


def call_qkv_grads(idx, n1t, gg, *parts):
    length = n1t.shape[1]
    s = jax.ShapeDtypeStruct
    return pl.pallas_call(
        qkv_grads,
        out_shape=[s((QUAD, QUAD, QKV_ROWS, DB), BF16)] + [s((QUAD, QKV_ROWS, DB), BF16)] * QUAD,
        grid_spec=pltpu.PrefetchScalarGridSpec(
            num_scalar_prefetch=1,
            grid=(QUAD,),
            in_specs=[
                pl.BlockSpec((D, length), lambda i, p: (0, 0)),
                pl.BlockSpec((QUAD, 8, DB), lambda i, p: (0, 0, 0)),
            ]
            + [pl.BlockSpec(part.shape, lambda i, p: (0, 0, 0)) for part in parts],
            out_specs=[pl.BlockSpec((QUAD, 1, QKV_ROWS, DB), lambda i, p: (0, i, 0, 0))]
            + [pl.BlockSpec((1, QKV_ROWS, DB), lambda i, p: (i, 0, 0))] * QUAD,
            scratch_shapes=[
                pltpu.VMEM((D + 2 * KV_HEADS * HEAD_DIM, length), BF16),
                pltpu.VMEM((D, length), BF16),
                pltpu.VMEM((QKV, D), F32),
            ],
        ),
        compiler_params=params(),
        name="qkv_grads",
        cost_estimate=pl.CostEstimate(flops=300000000, bytes_accessed=1000000, transcendentals=0),
    )(idx, n1t, gg, *parts)


CORE = [(i, i ^ 1) for i in range(8)]
ALONG_X = [(i, i ^ 2) for i in range(8)]
ALONG_Y = [(i, i ^ 4) for i in range(8)]
ACROSS = [(i, i ^ 6) for i in range(8)]


def swap(values):
    return lax.ppermute(values, "fsdp", CORE)


def from_z(values, k):
    return lax.ppermute(values, "dp", [(j, (j - k) % QUAD) for j in range(QUAD)])


def to_z(values, k):
    return lax.ppermute(values, "dp", [(j, (j + k) % QUAD) for j in range(QUAD)])


def spread_z(piece):
    return (piece,) + tuple(from_z(piece, k) for k in range(1, QUAD))


def spread_sides(own):
    return (own, lax.ppermute(own, "fsdp", ALONG_X), lax.ppermute(own, "fsdp", ALONG_Y))


def spread_across(own, by_x, by_y):
    return (lax.ppermute(by_y[:2], "fsdp", ALONG_X), lax.ppermute(by_x[2:], "fsdp", ALONG_Y))


def spread_core(pieces):
    return tuple(swap(piece) for piece in pieces)


def add(parts):
    return functools.reduce(jnp.add, [part.astype(F32) for part in parts])


def swap_plane(blocks):
    return (
        blocks[0],
        lax.ppermute(blocks[1], "fsdp", ALONG_X),
        lax.ppermute(blocks[2], "fsdp", ALONG_Y),
        lax.ppermute(blocks[3], "fsdp", ACROSS),
    )


def swap_corner(block):
    half = block.shape[0] // 2
    return (lax.ppermute(block[:half], "fsdp", ALONG_X), lax.ppermute(block[half:], "fsdp", ALONG_Y))


def swap_sides(blocks, corner):
    half = blocks[1].shape[0] // 2
    to_x = jnp.concatenate([blocks[1][:half], add([blocks[1][half:], corner[1]]).astype(BF16)], axis=0)
    to_y = jnp.concatenate([add([blocks[2][:half], corner[0]]).astype(BF16), blocks[2][half:]], axis=0)
    return (blocks[0], lax.ppermute(to_x, "fsdp", ALONG_X), lax.ppermute(to_y, "fsdp", ALONG_Y))


def swap_z(blocks):
    return (blocks[0],) + tuple(to_z(blocks[k], k) for k in range(1, QUAD))


def slab(values, start, size, axis):
    return lax.dynamic_slice_in_dim(values, start, size, axis)


def tables(yx, z, core, first):
    entries = [yx ^ k for k in range(QUAD)] + [(z + k) % QUAD for k in range(QUAD)]
    entries += [core, first, 1 - core, 0, 0, 0, 0, 0]
    return jnp.stack([jnp.asarray(e, jnp.int32) for e in entries])


def gather_near(core, early, gain_attn, w_query, w_key, w_value, w_out, gain_mlp, w_gate, w_up, w_down):
    zero = core == 0
    rows = jnp.concatenate([w_out, w_query, w_key, w_value], axis=1)
    share = rows.shape[0]
    extra = ROWS - share
    pad = jnp.zeros((1, 256 - DB), BF16)
    gains = jnp.concatenate(
        [gain_attn[None], jnp.zeros((1, 256 - share), BF16), gain_mlp[None], jnp.zeros((1, FB - 256 - share), BF16)], axis=1
    )
    sent = jnp.concatenate([rows[0:extra], gains, jnp.zeros((SPARE - extra - 1, FB), BF16)], axis=0)
    taken = swap(sent)
    theirs = taken[extra : extra + 1]
    line = jnp.concatenate(
        [theirs[:, 0:share], gain_attn[None], pad, theirs[:, 256 : 256 + share], gain_mlp[None], jnp.zeros((1, FB - 256 - DB), BF16)],
        axis=1,
    )
    attn = jnp.where(
        zero,
        jnp.concatenate([rows, taken[0:extra]], axis=0),
        jnp.concatenate([jnp.broadcast_to(line, (SPARE, FB)), rows[extra:]], axis=0),
    )
    turned = w_down.T
    taken = swap(slab(turned, (1 - core) * (DB - ROWS), ROWS, 0))
    kept = slab(turned, core * (DB - ROWS), ROWS, 0)
    down = jnp.where(zero, jnp.concatenate([kept, taken], axis=1), jnp.concatenate([taken, kept], axis=1))
    taken = swap(jnp.where(zero, w_up, w_gate))
    pair = jnp.where(zero, jnp.concatenate([w_gate, taken], axis=0), jnp.concatenate([taken, w_up], axis=0))
    near_z = (from_z(pair, 1), from_z(pair, 3))
    attn = jnp.stack(spread_z(attn) + (down,))
    attn, early = lax.optimization_barrier((attn, early))
    sides = spread_sides(attn)
    other = swap(attn)
    sides, other, near_z, own = lax.optimization_barrier((sides, other, near_z, pair))
    across = spread_across(*sides)
    pair = (pair, near_z[0], from_z(own, 2), near_z[1])
    across, pair, sides = lax.optimization_barrier((across, pair, sides))
    return sides + across, other, pair, early


def after(values, *others):
    return lax.optimization_barrier((values, others))[0]


def in_pieces(blocks):
    return (blocks[0], blocks[1], blocks[2], blocks[3, 0:2], blocks[3, 2:4])


def gather_any(gain_attn, w_query, w_key, w_value, w_out, gain_mlp, w_gate, w_up, w_down):
    def whole(weight):
        return lax.all_gather(lax.all_gather(weight, "dp", axis=1, tiled=True), "fsdp", axis=0, tiled=True)

    def blocks(weight):
        return weight.reshape(QUAD, weight.shape[0] // QUAD, QUAD, weight.shape[1] // QUAD).transpose(0, 2, 1, 3)

    attn = jnp.concatenate([blocks(whole(w)) for w in (w_out, w_query, w_key, w_value)], axis=3)
    gains = [lax.all_gather(g, "fsdp", axis=0, tiled=True).reshape(QUAD, 1, 1, DB) for g in (gain_attn, gain_mlp)]
    line = jnp.concatenate(
        [gains[0], jnp.zeros((QUAD, 1, 1, 256 - DB), BF16), gains[1], jnp.zeros((QUAD, 1, 1, FB - 256 - DB), BF16)], axis=3
    )
    line = jnp.broadcast_to(line, (QUAD, QUAD, SPARE, FB))
    attn_two = jnp.concatenate([line, attn[:, :, ROWS:]], axis=2)
    down = blocks(whole(w_down).T).transpose(1, 0, 2, 3)
    pair = [in_pieces(blocks(whole(w))) for w in (w_gate, w_up)]
    return (
        in_pieces(attn[:, :, 0:ROWS]) + in_pieces(attn_two),
        pair[0] + pair[1],
        tuple(down[:, z, 0:ROWS] for z in range(QUAD)) + tuple(down[:, z, DB - ROWS :] for z in range(QUAD)),
    )


def on_device(
    near,
    tokens,
    first_len,
    gain_attn,
    w_query,
    w_key,
    w_value,
    w_out,
    gain_mlp,
    w_gate,
    w_up,
    w_down,
    cotangent,
):
    length = tokens.shape[0]
    first = first_len[0]
    weights = (gain_attn, w_query, w_key, w_value, w_out, gain_mlp, w_gate, w_up, w_down)
    if near:
        place = lax.axis_index("fsdp")
        core = place & 1
        idx = tables(place >> 1, lax.axis_index("dp"), core, first)
        attn, other, pair, (idx, cosine, sine) = gather_near(core, (idx, *rope_tables(first, length)), *weights)
    else:
        core = 0
        idx = tables(0, 0, 0, first)
        attn, pair, down = gather_any(*weights)
        cosine, sine = rope_tables(first, length)
    xt, ct = tokens.T, cotangent.T
    if near:
        down = jnp.stack([attn[0][QUAD], attn[1][QUAD], attn[2][QUAD], attn[4][2]])
        attn = attn + (other,) + spread_core(attn[1:])
        pair = jnp.stack(pair)
        attn, pair, down = lax.optimization_barrier((attn, pair, down))
        pair = spread_sides(pair)
        pair_own = swap(pair[0])
        down = (down, from_z(down, 1))
    weight, gains, n1t, qx, kx, kt, vt = call_project(idx, xt, cosine, sine, attn)
    if near:
        down, pair_own, qx = lax.optimization_barrier((down, pair_own, qx))
        down = down + (from_z(down[1], 1),)
        down_core = spread_core(down[0:2])
    ot, lse = call_attend(qx, kx, vt)
    if near:
        pair, down, down_core, ot = lax.optimization_barrier((pair, down, down_core, ot))
        down = down + (from_z(down[2], 1),)
        pair = pair + spread_across(*pair)
        pair_core = (pair_own,) + spread_core(pair[1:3])
    y, n2, n2t = call_leave(xt, gains, weight, ot)
    if near:
        pair, pair_core, down, n2 = lax.optimization_barrier((pair, pair_core, down, n2))
        pair = pair + pair_core + spread_core(pair[3:5])
        down = down + down_core + spread_core(down[2:4])
    mixed, h, dgu, dyt, dat, gain_two = call_feed(idx, n2, y, ct, gains, pair, down)

    halves = gain_two[0].reshape(QUAD, 1, 2, DB // 2)
    row = jnp.pad(halves, ((0, 0), (0, 7), (0, 0), (0, FB // 2 - DB // 2))).reshape(QUAD, 8, FB)
    args_down = (ct, h, ot.reshape(D, length), dat, row)
    pair_theirs = call_pair_grads(idx, n2t, dgu)[0]
    if near:
        came = swap(pair_theirs)
        args_down = after(args_down, pair_theirs)
    else:
        came = jnp.zeros_like(pair_theirs)
    down_theirs = call_down_grads(idx, *args_down)[0]
    if near:
        came_down = swap(down_theirs)
        came = after(came, down_theirs)
    else:
        came_down = jnp.zeros_like(down_theirs)
    pair_mine = call_pair_grads(idx, n2t, dgu, received=came)
    if near:
        pair_got = swap_plane(pair_mine)
        came_down = after(came_down, pair_mine)
    down_mine = call_down_grads(idx, *args_down, received=came_down)
    if near:
        down_mine, dat = lax.optimization_barrier((down_mine, dat))
        down_corner = swap_corner(down_mine[3])
    do = call_give(weight, dat)
    heads = (qx, kx, kt, vt, ot, do, lse, cosine, sine)
    first_part = call_attend_backward(0, 2, *heads)
    if near:
        heads = after(heads, first_part)
    second_part = call_attend_backward(2, 3, *heads)
    if near:
        pair_got, down_corner, second_part = lax.optimization_barrier((pair_got, down_corner, second_part))
        pair_got = swap_z(add(pair_got).astype(BF16))
        down_got = swap_sides(down_mine, down_corner)
    parts = first_part + second_part
    grad_tokens, gain_one = call_enter_backward(idx, xt, dyt, gains, weight, *parts)
    qkv_theirs, *qkv_mine = call_qkv_grads(idx, n1t, gain_one, *parts)
    if near:
        pair_got, down_got, qkv_theirs = lax.optimization_barrier((pair_got, down_got, qkv_theirs))
        came = swap(qkv_theirs)
        qkv_got = swap_plane([add([part, came[k]]).astype(BF16) for k, part in enumerate(qkv_mine)])
        down_got = swap_z(add(down_got).astype(BF16))
        pair_sum = add(pair_got)
        qkv_got, down_got, pair_sum = lax.optimization_barrier((qkv_got, down_got, pair_sum))
        qkv_got = swap_z(add(qkv_got).astype(BF16))
        down_sum, qkv_sum = add(down_got), add(qkv_got)
        outs = settle_near(core, down_sum, pair_sum, qkv_sum)
    else:
        outs = settle_any(
            down_mine, down_theirs, pair_mine, pair_theirs, qkv_mine, qkv_theirs, gain_one[:, 0].reshape(D), gain_two[0]
        )
    return (mixed.T, grad_tokens.T) + outs


def settle_near(core, down_sum, pair_sum, qkv_sum):
    zero = core == 0
    share = DB // 2

    kept = slab(pair_sum, core * share, share, 0)
    taken = swap(slab(pair_sum, (1 - core) * share, share, 0).astype(BF16)).astype(F32)
    grad_gate, grad_up = jnp.where(zero, kept, taken), jnp.where(zero, taken, kept)

    grad_out = jnp.where(zero, down_sum[0:share, FB : FB + DB], down_sum[ROWS - share :, FB : FB + DB])
    half = FB // 2
    kept = slab(down_sum, core * half, half, 1)
    taken = swap(slab(down_sum, (1 - core) * half, half, 1).astype(BF16)).astype(F32)
    upper, lower = jnp.where(zero, kept, taken), jnp.where(zero, taken, kept)
    grad_down = jnp.concatenate([upper, lower[SPARE:]], axis=0).T
    grad_gain_mlp = lower[0, 0:share]

    kept = slab(qkv_sum, core * share, share, 1)
    taken = swap(slab(qkv_sum, (1 - core) * share, share, 1).astype(BF16)).astype(F32)
    upper, lower = jnp.where(zero, kept, taken), jnp.where(zero, taken, kept)
    grad_gain_attn = lower[0]
    rows = jnp.concatenate([upper, lower[SPARE:]], axis=0).T
    return (
        grad_gain_attn, rows[:, 0:QB], rows[:, QB : QB + KB], rows[:, QB + KB :], grad_out,
        grad_gain_mlp, grad_gate, grad_up, grad_down,
    )


def settle_any(down_mine, down_theirs, pair_mine, pair_theirs, qkv_mine, qkv_theirs, gain_one, gain_two):
    def whole(blocks):
        return blocks.transpose(0, 2, 1, 3).reshape(blocks.shape[0] * blocks.shape[2], -1)

    def shard(values):
        values = lax.psum_scatter(values, "fsdp", scatter_dimension=0, tiled=True)
        return lax.psum_scatter(values, "dp", scatter_dimension=1, tiled=True).astype(F32)

    def gain(values):
        values = lax.psum(values, "dp")
        return lax.psum_scatter(values, "fsdp", scatter_dimension=0, tiled=True)

    both = jnp.concatenate([jnp.stack(down_mine), down_theirs[:, :, SPARE:]], axis=2)
    grad_down = shard(whole(both[..., 0:FB].transpose(1, 0, 2, 3)).T)
    grad_out = shard(whole(both[..., FB : FB + DB]))
    grad_gate, grad_up = shard(whole(jnp.stack(pair_mine))), shard(whole(pair_theirs))
    both = jnp.concatenate([jnp.stack(qkv_mine), qkv_theirs[:, :, SPARE:]], axis=2).transpose(0, 1, 3, 2)
    grad_query = shard(whole(both[..., 0:QB]))
    grad_key = shard(whole(both[..., QB : QB + KB]))
    grad_value = shard(whole(both[..., QB + KB :]))
    return (
        gain(gain_one), grad_query, grad_key, grad_value, grad_out, gain(gain_two), grad_gate, grad_up, grad_down,
    )


def solution(mesh):
    sizes = dict(mesh.shape)
    near = sizes["fsdp"] == 8 and sizes["dp"] == QUAD
    in_specs = (
        P(("fsdp", "dp"), None),
        P(("fsdp", "dp")),
        P("fsdp"),
        P("fsdp", "dp"),
        P("fsdp", "dp"),
        P("fsdp", "dp"),
        P("fsdp", "dp"),
        P("fsdp"),
        P("fsdp", "dp"),
        P("fsdp", "dp"),
        P("fsdp", "dp"),
        P(("fsdp", "dp"), None),
    )
    out_specs = (
        P(("fsdp", "dp"), None),
        P(("fsdp", "dp"), None),
        P("fsdp"),
        P("fsdp", "dp"),
        P("fsdp", "dp"),
        P("fsdp", "dp"),
        P("fsdp", "dp"),
        P("fsdp"),
        P("fsdp", "dp"),
        P("fsdp", "dp"),
        P("fsdp", "dp"),
    )
    return jax.shard_map(
        functools.partial(on_device, near), mesh=mesh, in_specs=in_specs, out_specs=out_specs, check_vma=False
    )
```

```python
import functools

import jax
import jax.numpy as jnp
from jax import lax
from jax.experimental import pallas as pl
from jax.experimental.pallas import tpu as pltpu
from jax.sharding import PartitionSpec as P

D = 960
FF = 2560
HEADS = 15
KV_HEADS = 5
GROUP = HEADS // KV_HEADS
HEAD_DIM = 64
HALF = HEAD_DIM // 2
TILE = 256
QUAD = 4
DB = D // QUAD
FB = FF // QUAD
QB = D // QUAD
KB = KV_HEADS * HEAD_DIM // QUAD
ROWS = 128
SPARE = 16
QKV = QB + 2 * KB
QKV_ROWS = 208
LEAD = FB - 512
SKIP = DB - LEAD
NEG = -1e30
EPS = 1e-05
ROPE_BASE = 10000.0
BIG = 60 * 1024 * 1024

F32 = jnp.float32
BF16 = jnp.bfloat16


def nn(a, b):
    return jnp.dot(a, b, preferred_element_type=F32)


def nt(a, b):
    return lax.dot_general(a, b, (((1,), (1,)), ((), ())), preferred_element_type=F32)


def rope_tables(first, length):
    places = jnp.arange(length, dtype=jnp.int32)
    position = jnp.where(places < first, places, places - first).astype(F32)
    frequency = ROPE_BASE ** (-jnp.arange(0, HEAD_DIM, 2, dtype=F32) / HEAD_DIM)
    angles = frequency[:, None] * position[None, :]
    return jnp.cos(angles), jnp.sin(angles)


def params():
    return pltpu.CompilerParams(vmem_limit_bytes=BIG)


def any_spec():
    return pl.BlockSpec(memory_space=pl.ANY)


def by_plane_halved(pieces, k, kz):
    if k < 3:
        return pieces[k].at[kz]
    return pieces[3 + kz // 2].at[kz % 2]


def by_z(pieces, k, kz):
    return pieces[kz].at[k]


def copies(idx, pieces, pick, sems, target):
    plans = ([], [])
    mine, other = pieces[: len(pieces) // 2], pieces[len(pieces) // 2 :]
    for mine_core in range(2):
        slot = 0
        for core, found in ((mine_core, mine), (1 - mine_core, other)):
            for k in range(QUAD):
                for kz in range(QUAD):
                    ref = pick(found, k, kz)
                    for source, dest in target(core, idx[4 + kz], idx[k], kz):
                        src = ref if source is None else ref.at[pl.ds(*source), :]
                        plans[mine_core].append(
                            pltpu.make_async_copy(src, dest, sems.at[slot])
                        )
                        slot += 1
    return plans


def rows_target(weight, gains=None):
    def target(core, z, yx, kz):
        base = pl.multiple_of(yx * DB, 16)
        if core == 0:
            return [((0, ROWS), weight.at[z, pl.ds(base, ROWS), :])]
        found = [((SPARE, DB - ROWS), weight.at[z, pl.ds(base + ROWS, DB - ROWS), :])]
        if gains is not None and kz == 0:
            found.append(((0, SPARE), gains.at[yx]))
        return found

    return target


def down_target(weight):
    def target(core, z, yx, kz):
        base = pl.multiple_of(z * DB, 16)
        columns = pl.ds(pl.multiple_of(yx * FB, 128), FB)
        if core == 0:
            return [((0, ROWS), weight.at[pl.ds(base, ROWS), columns])]
        return [((SPARE, DB - ROWS), weight.at[pl.ds(base + ROWS, DB - ROWS), columns])]

    return target


def pair_target(weight):
    def target(core, z, yx, kz):
        base = pl.multiple_of(yx * DB, 16)
        columns = pl.ds(pl.multiple_of(z * FB, 128), FB)
        return [(None, weight.at[core, pl.ds(base, DB), columns])]

    return target


def run_copies(core, plans):
    for c in range(2):

        @pl.when(core == c)
        def _():
            for copy in plans[c]:
                copy.start()
            for copy in plans[c]:
                copy.wait()


def norm_columns(x, axis):
    return lax.rsqrt(jnp.mean(x * x, axis=axis, keepdims=True) + EPS)


def column(row):
    return jnp.broadcast_to(row, (128, row.shape[1])).T[:, 0:1]


def project(idx, xt_ref, cos_ref, sin_ref, *rest):
    weight, gain_ref, n1t_ref, qx_ref, kx_ref, kt_ref, vt_ref, gains, sems = rest[10:]
    run_copies(idx[8], copies(idx, rest[0:10], by_plane_halved, sems, rows_target(weight, gains)))
    length = xt_ref.shape[1]
    first = idx[9]
    gain_one = jnp.concatenate([gains[b, 0:1, 0:DB] for b in range(QUAD)], axis=1).astype(F32)
    gain_two = jnp.concatenate([gains[b, 0:1, 256 : 256 + DB] for b in range(QUAD)], axis=1).astype(F32)
    gain_ref[0:1, :] = gain_one
    gain_ref[1:2, :] = gain_two
    gain_column = column(gain_one)

    place = lax.broadcasted_iota(jnp.int32, (HEAD_DIM, length), 1)
    row = lax.broadcasted_iota(jnp.int32, (HEAD_DIM, length), 0)
    extra_q = jnp.where((row == 0) & (place >= first), NEG, 0.0).astype(BF16)
    extra_k = jnp.where((row == 0) & (place < first), 1.0, 0.0)
    for h in range(HEADS):
        qx_ref[h, HEAD_DIM:, :] = extra_q

    def tile(i, carry):
        at = pl.ds(pl.multiple_of(i * FEED_TILE, FEED_TILE), FEED_TILE)
        x = xt_ref[:, at].astype(F32)
        n1t = (x * norm_columns(x, 0) * gain_column).astype(BF16)
        n1t_ref[:, at] = n1t
        n1 = n1t.T
        cosine, sine = cos_ref[:, at], sin_ref[:, at]
        flat = [nn(n1, weight[z, :, LEAD:]).T for z in range(QUAD)]
        queries = jnp.concatenate([f[SKIP : SKIP + QB] for f in flat], axis=0)
        keys = jnp.concatenate([f[SKIP + QB : SKIP + QB + KB] for f in flat], axis=0)
        values = jnp.concatenate([f[SKIP + QB + KB :] for f in flat], axis=0)

        def turn(u):
            u1, u2 = u[:HALF], u[HALF:]
            return jnp.concatenate([u1 * cosine - u2 * sine, u2 * cosine + u1 * sine], axis=0).astype(BF16)

        for h in range(HEADS):
            qx_ref[h, 0:HEAD_DIM, at] = turn(queries[h * HEAD_DIM : (h + 1) * HEAD_DIM]) * jnp.asarray(0.125, BF16)
        for h in range(KV_HEADS):
            kt_ref[h, :, at] = turn(keys[h * HEAD_DIM : (h + 1) * HEAD_DIM])
        vt_ref[:, :, at] = values.astype(BF16).reshape(KV_HEADS, HEAD_DIM, FEED_TILE)
        return carry

    lax.fori_loop(0, length // FEED_TILE, tile, 0)
    for j in range(KV_HEADS):
        wide = jnp.concatenate([kt_ref[j].astype(F32), extra_k], axis=0)
        kx_ref[j] = wide.T.astype(BF16)


def call_project(idx, xt, cosine, sine, pieces):
    length = xt.shape[1]
    s = jax.ShapeDtypeStruct
    vm = pl.BlockSpec(memory_space=pltpu.VMEM)
    return pl.pallas_call(
        project,
        out_shape=(
            s((QUAD, D, FB), BF16),
            s((8, D), F32),
            s((D, length), BF16),
            s((HEADS, 2 * HEAD_DIM, length), BF16),
            s((KV_HEADS, length, 2 * HEAD_DIM), BF16),
            s((KV_HEADS, HEAD_DIM, length), BF16),
            s((KV_HEADS, HEAD_DIM, length), BF16),
        ),
        in_specs=[pl.BlockSpec(memory_space=pltpu.SMEM)] + [vm] * 3 + [any_spec()] * 10,
        out_specs=(vm,) * 7,
        scratch_shapes=[
            pltpu.VMEM((QUAD, SPARE, FB), BF16),
            pltpu.SemaphoreType.DMA((64,)),
        ],
        compiler_params=params(),
        name="project",
        cost_estimate=pl.CostEstimate(flops=600000000, bytes_accessed=2000000, transcendentals=0),
    )(idx, xt, cosine, sine, *pieces)


def causal_mask():
    return lax.broadcasted_iota(jnp.int32, (TILE, GROUP * TILE), 0) > (
        lax.broadcasted_iota(jnp.int32, (TILE, GROUP * TILE), 1) % TILE
    )


def attend(qx_ref, kx_ref, vt_ref, ot_ref, lse_ref, raw_s, p_s):
    tiles = qx_ref.shape[2] // TILE
    causal = causal_mask()
    for b in range(tiles):
        at = slice(b * TILE, (b + 1) * TILE)
        span = (b + 1) * TILE
        qx = jnp.concatenate([qx_ref[g, :, at] for g in range(GROUP)], axis=1)
        raw_s[0:span, :] = nn(kx_ref[0, 0:span, :], qx)
        raw_s[at, :] = jnp.where(causal, NEG, raw_s[at, :])
        highest = jnp.max(raw_s[0:span, :], axis=0, keepdims=True)
        total = 0.0
        for s in range(b + 1):
            keys = slice(s * TILE, (s + 1) * TILE)
            weights = jnp.exp(raw_s[keys, :] - highest)
            total = total + jnp.sum(weights, axis=0, keepdims=True)
            p_s[keys, :] = weights.astype(BF16)
        out = nn(vt_ref[0, :, 0:span], p_s[0:span, :]) / total
        lse_ref[0, b] = highest + jnp.log(total)
        for g in range(GROUP):
            ot_ref[g, :, at] = out[:, g * TILE : (g + 1) * TILE].astype(BF16)


def heads_spec(count, rows, length):
    return pl.BlockSpec((count, rows, length), lambda j: (j, 0, 0))


def call_attend(qx, kx, vt):
    length = qx.shape[2]
    tiles = length // TILE
    s = jax.ShapeDtypeStruct
    return pl.pallas_call(
        attend,
        out_shape=(
            s((HEADS, HEAD_DIM, length), BF16),
            s((KV_HEADS, tiles, 1, GROUP * TILE), F32),
        ),
        grid=(KV_HEADS,),
        in_specs=[
            heads_spec(GROUP, 2 * HEAD_DIM, length),
            heads_spec(1, length, 2 * HEAD_DIM),
            heads_spec(1, HEAD_DIM, length),
        ],
        out_specs=[
            heads_spec(GROUP, HEAD_DIM, length),
            pl.BlockSpec((1, tiles, 1, GROUP * TILE), lambda j: (j, 0, 0, 0)),
        ],
        scratch_shapes=[
            pltpu.VMEM((length, GROUP * TILE), F32),
            pltpu.VMEM((length, GROUP * TILE), BF16),
        ],
        compiler_params=params(),
        name="attend",
        cost_estimate=pl.CostEstimate(flops=2000000000, bytes_accessed=800000, transcendentals=0),
    )(qx, kx, vt)


def leave(xt_ref, gain_ref, weight, ot_ref, y_ref, n2_ref, n2t_ref):
    o = ot_ref[...].reshape(D, ot_ref.shape[2]).T
    added = jnp.concatenate([nn(o, weight[z])[:, 0:DB] for z in range(QUAD)], axis=1)
    y = xt_ref[...].T.astype(F32) + added
    y_ref[...] = y
    n2 = (y * norm_columns(y, -1) * gain_ref[1:2, :]).astype(BF16)
    n2_ref[...] = n2
    n2t_ref[...] = n2.T


def call_leave(xt, gains, weight, ot):
    length = xt.shape[1]
    s = jax.ShapeDtypeStruct
    tall = pl.BlockSpec((D, FEED_TILE), lambda i: (0, i))
    wide = pl.BlockSpec((FEED_TILE, D), lambda i: (i, 0))
    return pl.pallas_call(
        leave,
        out_shape=(s((length, D), F32), s((length, D), BF16), s((D, length), BF16)),
        grid=(length // FEED_TILE,),
        in_specs=[
            tall,
            pl.BlockSpec((8, D), lambda i: (0, 0)),
            pl.BlockSpec((QUAD, D, 256), lambda i: (0, 0, 0)),
            pl.BlockSpec((HEADS, HEAD_DIM, FEED_TILE), lambda i: (0, 0, i)),
        ],
        out_specs=[wide, wide, tall],
        compiler_params=params(),
        name="leave",
        cost_estimate=pl.CostEstimate(flops=300000000, bytes_accessed=1500000, transcendentals=0),
    )(xt, gains, weight, ot)


def feed(idx, n2_ref, y_ref, ct_ref, gain_ref, *rest):
    pairs, downs = rest[0:10], rest[10:18]
    mixed_ref, h_ref, dgu_ref, dyt_ref, dat_ref, gg_ref, weight, down, sems = rest[18:]

    @pl.when(pl.program_id(0) == 0)
    def _():
        first = copies(idx, pairs, by_plane_halved, sems.at[0], pair_target(weight))
        second = copies(idx, downs, by_z, sems.at[1], down_target(down))
        run_copies(idx[8], [a + b for a, b in zip(first, second)])
        gg_ref[...] = jnp.zeros_like(gg_ref)

    n2 = n2_ref[...]
    chunks = [slice(b, b + FEED_CHUNK) for b in range(0, FF, FEED_CHUNK)]
    for at in chunks:
        g = nn(n2, weight[0, :, at])
        u = nn(n2, weight[1, :, at])
        sig = 1.0 / (1.0 + jnp.exp(-g))
        silu = g * sig
        h_ref[:, at] = (silu * u).astype(BF16)
        dgu_ref[0, :, at] = (u * (sig + silu * (1.0 - sig))).astype(BF16)
        dgu_ref[1, :, at] = silu.astype(BF16)
    y = y_ref[...]
    mixed_ref[...] = (y + nt(h_ref[...], down[...])).astype(BF16).T
    c = ct_ref[...].T
    for at in chunks:
        dh = nn(c, down[:, at])
        dgu_ref[0, :, at] = (dh * dgu_ref[0, :, at].astype(F32)).astype(BF16)
        dgu_ref[1, :, at] = (dh * dgu_ref[1, :, at].astype(F32)).astype(BF16)
    dn2 = nt(dgu_ref[0], weight[0]) + nt(dgu_ref[1], weight[1])
    r = norm_columns(y, -1)
    yr = y * r
    gg_ref[0:1, :] += jnp.sum(dn2 * yr, axis=0, keepdims=True)
    t = dn2 * gain_ref[1:2, :]
    dy = c.astype(F32) + r * (t - yr * jnp.mean(t * yr, axis=-1, keepdims=True))
    dyt = dy.T
    dyt_ref[...] = dyt
    dat_ref[...] = dyt.astype(BF16)


FEED_TILE = 512
FEED_CHUNK = 512


def call_feed(idx, n2, y, ct, gains, pairs, downs):
    length = n2.shape[0]
    s = jax.ShapeDtypeStruct
    wide = pl.BlockSpec((FEED_TILE, D), lambda i, p: (i, 0))
    tall = pl.BlockSpec((D, FEED_TILE), lambda i, p: (0, i))
    whole = pl.BlockSpec((8, D), lambda i, p: (0, 0))
    return pl.pallas_call(
        feed,
        out_shape=(
            s((D, length), BF16),
            s((length, FF), BF16),
            s((2, length, FF), BF16),
            s((D, length), F32),
            s((D, length), BF16),
            s((8, D), F32),
        ),
        grid_spec=pltpu.PrefetchScalarGridSpec(
            num_scalar_prefetch=1,
            grid=(length // FEED_TILE,),
            in_specs=[wide, wide, tall, whole] + [any_spec()] * 18,
            out_specs=[
                tall,
                pl.BlockSpec((FEED_TILE, FF), lambda i, p: (i, 0)),
                pl.BlockSpec((2, FEED_TILE, FF), lambda i, p: (0, i, 0)),
                tall,
                tall,
                whole,
            ],
            scratch_shapes=[
                pltpu.VMEM((2, D, FF), BF16),
                pltpu.VMEM((D, FF), BF16),
                pltpu.SemaphoreType.DMA((2, 64)),
            ],
        ),
        compiler_params=params(),
        name="feed_forward_backward",
        cost_estimate=pl.CostEstimate(flops=3000000000, bytes_accessed=5000000, transcendentals=0),
    )(idx, n2, y, ct, gains, *pairs, *downs)


def pair_grads(target, idx, n2t_ref, d_ref, *rest):
    full = rest[-1]
    received, outs = (rest[0:1], rest[1:-1]) if target == 0 else ((), rest[:-1])
    full[...] = nn(n2t_ref[...], d_ref[...])
    for k in range(QUAD):
        got = full[pl.ds(pl.multiple_of(idx[k] * DB, 16), DB), :]
        if received:
            got = got + received[0][k, 0].astype(F32)
        if len(outs) == 1:
            outs[0][k, 0] = got.astype(BF16)
        else:
            outs[k][0] = got.astype(BF16)


def call_pair_grads(idx, n2t, dgu, received=None):
    length = n2t.shape[1]
    s = jax.ShapeDtypeStruct
    block = pl.BlockSpec((QUAD, 1, DB, FB), lambda i, p: (0, i, 0, 0))
    matrix = 10 if received is None else 8
    specs = [
        pl.BlockSpec((D, length), lambda i, p: (0, 0)),
        pl.BlockSpec((None, length, FB), lambda i, p: (p[matrix], 0, p[4 + i])),
    ]
    if received is None:
        out_shape = [s((QUAD, QUAD, DB, FB), BF16)]
        out_specs = [block]
        extra = ()
    else:
        specs.append(block)
        extra = (received,)
        out_shape = [s((QUAD, DB, FB), BF16)] * QUAD
        out_specs = [pl.BlockSpec((1, DB, FB), lambda i, p: (i, 0, 0))] * QUAD
    return pl.pallas_call(
        functools.partial(pair_grads, 1 if received is None else 0),
        out_shape=out_shape,
        grid_spec=pltpu.PrefetchScalarGridSpec(
            num_scalar_prefetch=1,
            grid=(QUAD,),
            in_specs=specs,
            out_specs=out_specs,
            scratch_shapes=[pltpu.VMEM((D, FB), F32)],
        ),
        compiler_params=params(),
        name="pair_grads",
        cost_estimate=pl.CostEstimate(flops=500000000, bytes_accessed=1500000, transcendentals=0),
    )(idx, n2t, dgu, *extra)


WIDE = FB + 256


def down_grads(which, idx, ct_ref, h_ref, ot_ref, dat_ref, gg_ref, *rest):
    right, also = rest[-2:]
    received, outs = (rest[0:1], rest[1:-2]) if which == 8 else ((), rest[:-2])
    core = idx[which]
    k = pl.program_id(0)
    yx = idx[k]
    offset = core * (DB - ROWS)

    def rows(ref, block, size, shift):
        return ref[pl.ds(pl.multiple_of(block * DB + shift, 16), size), :]

    @pl.when(k == 0)
    def _():
        for kz in range(QUAD):
            right[kz * DB : (kz + 1) * DB, :] = rows(dat_ref, idx[4 + kz], DB, 0)
        left = jnp.concatenate([rows(ot_ref, idx[i], ROWS, offset) for i in range(QUAD)], axis=0)
        also[...] = nt(left, right[...]).reshape(QUAD, ROWS, D)

    left = jnp.concatenate([rows(ct_ref, idx[4 + kz], ROWS, offset) for kz in range(QUAD)], axis=0)
    full = nn(left, h_ref[...])
    spare = jnp.broadcast_to(gg_ref[yx, 0:1, :], (SPARE, FB))

    def put(ref, kz):
        got = full[kz * ROWS : (kz + 1) * ROWS]
        out = also[k, :, kz * DB : (kz + 1) * DB]
        head = jnp.where(core == 1, spare, got[0:SPARE])
        if received:
            got = got + received[0][0, kz, :, 0:FB].astype(F32)
            out = out + received[0][0, kz, :, FB : FB + DB].astype(F32)
            head = head + received[0][0, kz, 0:SPARE, 0:FB].astype(F32)
        ref[:, 0:FB] = got.astype(BF16)
        ref[:, FB : FB + DB] = out.astype(BF16)
        ref[:, FB + DB :] = jnp.zeros((ROWS, 256 - DB), BF16)
        ref[0:SPARE, 0:FB] = head.astype(BF16)

    if len(outs) == 1:
        for kz in range(QUAD):
            put(outs[0].at[0, kz], kz)
    else:
        for i in range(QUAD):

            @pl.when(k == i)
            def _():
                for kz in range(QUAD):
                    put(outs[i].at[kz], kz)


def call_down_grads(idx, ct, h, ot, dat, gg, received=None):
    length = ct.shape[1]
    s = jax.ShapeDtypeStruct
    block = pl.BlockSpec((1, QUAD, ROWS, WIDE), lambda i, p: (i, 0, 0, 0))
    vm = pl.BlockSpec((D, length), lambda i, p: (0, 0))
    specs = [
        vm,
        pl.BlockSpec((length, FB), lambda i, p: (0, p[i])),
        vm,
        vm,
        pl.BlockSpec((QUAD, 8, FB), lambda i, p: (0, 0, 0)),
    ]
    if received is None:
        out_shape, out_specs, extra = [s((QUAD, QUAD, ROWS, WIDE), BF16)], [block], ()
    else:
        specs.append(block)
        extra = (received,)
        out_shape = [s((QUAD, ROWS, WIDE), BF16)] * QUAD
        out_specs = [pl.BlockSpec((QUAD, ROWS, WIDE), lambda i, p: (0, 0, 0))] * QUAD
    return pl.pallas_call(
        functools.partial(down_grads, 10 if received is None else 8),
        out_shape=out_shape,
        grid_spec=pltpu.PrefetchScalarGridSpec(
            num_scalar_prefetch=1,
            grid=(QUAD,),
            in_specs=specs,
            out_specs=out_specs,
            scratch_shapes=[pltpu.VMEM((D, length), BF16), pltpu.VMEM((QUAD, ROWS, D), F32)],
        ),
        compiler_params=params(),
        name="down_grads",
        cost_estimate=pl.CostEstimate(flops=400000000, bytes_accessed=1500000, transcendentals=0),
    )(idx, ct, h, ot, dat, gg, *extra)


def give(weight, dat_ref, do_ref):
    total = 0.0
    for z in range(QUAD):
        total = total + nn(weight[z, :, 0:DB], dat_ref[z * DB : (z + 1) * DB, :])
    do_ref[...] = total.astype(BF16).reshape(do_ref.shape)


def call_give(weight, dat):
    length = dat.shape[1]
    return pl.pallas_call(
        give,
        out_shape=jax.ShapeDtypeStruct((HEADS, HEAD_DIM, length), BF16),
        grid=(length // FEED_TILE,),
        in_specs=[
            pl.BlockSpec((QUAD, D, 256), lambda i: (0, 0, 0)),
            pl.BlockSpec((D, FEED_TILE), lambda i: (0, i)),
        ],
        out_specs=pl.BlockSpec((HEADS, HEAD_DIM, FEED_TILE), lambda i: (0, 0, i)),
        compiler_params=params(),
        name="give",
        cost_estimate=pl.CostEstimate(flops=200000000, bytes_accessed=600000, transcendentals=0),
    )(weight, dat)


def unrotate(grads, cosine, sine):
    u1, u2 = grads[:HALF], grads[HALF:]
    return jnp.concatenate([u1 * cosine + u2 * sine, u2 * cosine - u1 * sine], axis=0)


def attend_backward(
    qx_ref, kx_ref, kt_ref, vt_ref, ot_ref, do_ref, lse_ref, cos_ref, sin_ref, zq, zk, zv,
    dk_s, dv_s, raw_s, dp_s, p_s, ds_s,
):
    tiles = qx_ref.shape[2] // TILE
    causal = causal_mask()
    values = vt_ref[0].astype(F32).T.astype(BF16)
    for b in reversed(range(tiles)):
        at = slice(b * TILE, (b + 1) * TILE)
        span = (b + 1) * TILE
        qx = jnp.concatenate([qx_ref[g, :, at] for g in range(GROUP)], axis=1)
        do = jnp.concatenate([do_ref[g, :, at] for g in range(GROUP)], axis=1)
        o = jnp.concatenate([ot_ref[g, :, at] for g in range(GROUP)], axis=1)
        inner = jnp.sum(do.astype(F32) * o.astype(F32), axis=0, keepdims=True)
        log_total = lse_ref[0, b]
        raw_s[0:span, :] = nn(kx_ref[0, 0:span, :], qx)
        dp_s[0:span, :] = nn(values[0:span, :], do)
        for s in range(b + 1):
            keys = slice(s * TILE, (s + 1) * TILE)
            raw = raw_s[keys, :]
            if s == b:
                raw = jnp.where(causal, NEG, raw)
            probs = jnp.exp(raw - log_total)
            p_s[keys, :] = probs.astype(BF16)
            ds_s[keys, :] = (probs * (dp_s[keys, :] - inner)).astype(BF16)
        dq = nn(kt_ref[0, :, 0:span], ds_s[0:span, :])
        dk = nt(ds_s[0:span, :], qx[0:HEAD_DIM, :])
        dv = nt(p_s[0:span, :], do)
        if b == tiles - 1:
            dk_s[...] = dk
            dv_s[...] = dv
        else:
            dk_s[0:span, :] += dk
            dv_s[0:span, :] += dv
        cosine, sine = cos_ref[:, at], sin_ref[:, at]
        for g in range(GROUP):
            part = unrotate(dq[:, g * TILE : (g + 1) * TILE] * 0.125, cosine, sine)
            zq[g, :, at] = part.astype(BF16)
    zk[0] = unrotate(dk_s[...].T, cos_ref[...], sin_ref[...]).astype(BF16)
    zv[0] = dv_s[...].T.astype(BF16)


def call_attend_backward(start, count, qx, kx, kt, vt, ot, do, lse, cosine, sine):
    length = qx.shape[2]
    tiles = length // TILE
    s = jax.ShapeDtypeStruct

    def spec(heads, rows, lanes):
        return pl.BlockSpec((heads, rows, lanes), lambda j: (j + start, 0, 0))

    table = pl.BlockSpec((HALF, length), lambda j: (0, 0))
    return pl.pallas_call(
        attend_backward,
        out_shape=(
            s((GROUP * count, HEAD_DIM, length), BF16),
            s((count, HEAD_DIM, length), BF16),
            s((count, HEAD_DIM, length), BF16),
        ),
        grid=(count,),
        in_specs=[
            spec(GROUP, 2 * HEAD_DIM, length),
            spec(1, length, 2 * HEAD_DIM),
            spec(1, HEAD_DIM, length),
            spec(1, HEAD_DIM, length),
            spec(GROUP, HEAD_DIM, length),
            spec(GROUP, HEAD_DIM, length),
            pl.BlockSpec((1, tiles, 1, GROUP * TILE), lambda j: (j + start, 0, 0, 0)),
            table,
            table,
        ],
        out_specs=[
            heads_spec(GROUP, HEAD_DIM, length),
            heads_spec(1, HEAD_DIM, length),
            heads_spec(1, HEAD_DIM, length),
        ],
        scratch_shapes=[
            pltpu.VMEM((length, HEAD_DIM), F32),
            pltpu.VMEM((length, HEAD_DIM), F32),
            pltpu.VMEM((length, GROUP * TILE), F32),
            pltpu.VMEM((length, GROUP * TILE), F32),
            pltpu.VMEM((length, GROUP * TILE), BF16),
            pltpu.VMEM((length, GROUP * TILE), BF16),
        ],
        compiler_params=params(),
        name="attend_backward",
        cost_estimate=pl.CostEstimate(flops=1000000000, bytes_accessed=1000000, transcendentals=0),
    )(qx, kx, kt, vt, ot, do, lse, cosine, sine)


def enter_backward(idx, xt_ref, dyt_ref, gain_ref, weight, *rest):
    parts, (gx_ref, gg_ref, sums) = rest[:-3], rest[-3:]
    i = pl.program_id(0)

    @pl.when(i == 0)
    def _():
        sums[...] = jnp.zeros_like(sums)

    def flat(found):
        return jnp.concatenate([ref[...].reshape(-1, TILE) for ref in found], axis=0)

    zq, zk, zv = flat(parts[0::3]), flat(parts[1::3]), flat(parts[2::3])
    dn1 = 0.0
    for z in range(QUAD):
        block = jnp.concatenate(
            [
                jnp.zeros((SKIP, TILE), BF16),
                zq[z * QB : (z + 1) * QB],
                zk[z * KB : (z + 1) * KB],
                zv[z * KB : (z + 1) * KB],
            ],
            axis=0,
        )
        dn1 = dn1 + nn(weight[z, :, LEAD:], block)
    x = xt_ref[...].astype(F32)
    r = norm_columns(x, 0)
    xr = x * r
    found = dn1 * xr
    sums[...] += found[:, 0:128] + found[:, 128:256]
    t = dn1 * column(gain_ref[0:1, :])
    gx = dyt_ref[...] + r * (t - xr * jnp.mean(t * xr, axis=0, keepdims=True))
    gx_ref[...] = gx.astype(BF16)

    @pl.when(i == pl.num_programs(0) - 1)
    def _():
        for k in range(QUAD):
            rows = sums[pl.ds(pl.multiple_of(idx[k] * DB, 16), DB), :]
            gg_ref[k] = jnp.broadcast_to(jnp.sum(rows.T, axis=0, keepdims=True), (8, DB))


def call_enter_backward(idx, xt, dyt, gains, weight, *parts):
    length = xt.shape[1]
    s = jax.ShapeDtypeStruct
    tall = pl.BlockSpec((D, TILE), lambda i, p: (0, i))
    return pl.pallas_call(
        enter_backward,
        out_shape=(s((D, length), BF16), s((QUAD, 8, DB), F32)),
        grid_spec=pltpu.PrefetchScalarGridSpec(
            num_scalar_prefetch=1,
            grid=(length // TILE,),
            in_specs=[
                tall,
                tall,
                pl.BlockSpec((8, D), lambda i, p: (0, 0)),
                pl.BlockSpec((QUAD, D, FB), lambda i, p: (0, 0, 0)),
            ]
            + [pl.BlockSpec((part.shape[0], HEAD_DIM, TILE), lambda i, p: (0, 0, i)) for part in parts],
            out_specs=[tall, pl.BlockSpec((QUAD, 8, DB), lambda i, p: (0, 0, 0))],
            scratch_shapes=[pltpu.VMEM((D, 128), F32)],
        ),
        compiler_params=params(),
        name="enter_backward",
        cost_estimate=pl.CostEstimate(flops=400000000, bytes_accessed=1500000, transcendentals=0),
    )(idx, xt, dyt, gains, weight, *parts)


def qkv_grads(idx, n1t_ref, gg_ref, *rest):
    parts, (theirs, *mine), (flat, right, full) = rest[0:6], rest[6:-3], rest[-3:]

    @pl.when(pl.program_id(0) == 0)
    def _():
        at = 0
        for found in (parts[0::3], parts[1::3], parts[2::3]):
            for ref in found:
                rows = ref[...].reshape(-1, ref.shape[2])
                flat[at : at + rows.shape[0], :] = rows
                at += rows.shape[0]
        for k in range(QUAD):
            right[k * DB : (k + 1) * DB, :] = n1t_ref[pl.ds(pl.multiple_of(idx[k] * DB, 16), DB), :]

    z = idx[4 + pl.program_id(0)]
    width = KV_HEADS * HEAD_DIM
    left = jnp.concatenate(
        [
            flat[pl.ds(pl.multiple_of(z * QB, 16), QB), :],
            flat[pl.ds(pl.multiple_of(D + z * KB, 16), KB), :],
            flat[pl.ds(pl.multiple_of(D + width + z * KB, 16), KB), :],
        ],
        axis=0,
    )
    full[...] = nt(left, right[...])
    for which in (10, 8):
        part = full[pl.ds(pl.multiple_of(idx[which] * (QKV - QKV_ROWS), 16), QKV_ROWS), :]
        for k in range(QUAD):
            got = part[:, k * DB : (k + 1) * DB]
            spare = jnp.broadcast_to(gg_ref[k, 0:1, :], (SPARE, DB))
            ref = theirs.at[k, 0] if which == 10 else mine[k].at[0]
            ref[...] = got.astype(BF16)
            ref[0:SPARE, :] = jnp.where(idx[which] == 1, spare, got[0:SPARE]).astype(BF16)


def call_qkv_grads(idx, n1t, gg, *parts):
    length = n1t.shape[1]
    s = jax.ShapeDtypeStruct
    return pl.pallas_call(
        qkv_grads,
        out_shape=[s((QUAD, QUAD, QKV_ROWS, DB), BF16)] + [s((QUAD, QKV_ROWS, DB), BF16)] * QUAD,
        grid_spec=pltpu.PrefetchScalarGridSpec(
            num_scalar_prefetch=1,
            grid=(QUAD,),
            in_specs=[
                pl.BlockSpec((D, length), lambda i, p: (0, 0)),
                pl.BlockSpec((QUAD, 8, DB), lambda i, p: (0, 0, 0)),
            ]
            + [pl.BlockSpec(part.shape, lambda i, p: (0, 0, 0)) for part in parts],
            out_specs=[pl.BlockSpec((QUAD, 1, QKV_ROWS, DB), lambda i, p: (0, i, 0, 0))]
            + [pl.BlockSpec((1, QKV_ROWS, DB), lambda i, p: (i, 0, 0))] * QUAD,
            scratch_shapes=[
                pltpu.VMEM((D + 2 * KV_HEADS * HEAD_DIM, length), BF16),
                pltpu.VMEM((D, length), BF16),
                pltpu.VMEM((QKV, D), F32),
            ],
        ),
        compiler_params=params(),
        name="qkv_grads",
        cost_estimate=pl.CostEstimate(flops=300000000, bytes_accessed=1000000, transcendentals=0),
    )(idx, n1t, gg, *parts)


CORE = [(i, i ^ 1) for i in range(8)]
ALONG_X = [(i, i ^ 2) for i in range(8)]
ALONG_Y = [(i, i ^ 4) for i in range(8)]
ACROSS = [(i, i ^ 6) for i in range(8)]


def swap(values):
    return lax.ppermute(values, "fsdp", CORE)


def from_z(values, k):
    return lax.ppermute(values, "dp", [(j, (j - k) % QUAD) for j in range(QUAD)])


def to_z(values, k):
    return lax.ppermute(values, "dp", [(j, (j + k) % QUAD) for j in range(QUAD)])


def spread_z(piece):
    return (piece,) + tuple(from_z(piece, k) for k in range(1, QUAD))


def spread_sides(own):
    return (own, lax.ppermute(own, "fsdp", ALONG_X), lax.ppermute(own, "fsdp", ALONG_Y))


def spread_across(own, by_x, by_y):
    return (lax.ppermute(by_y[:2], "fsdp", ALONG_X), lax.ppermute(by_x[2:], "fsdp", ALONG_Y))


def spread_core(pieces):
    return tuple(swap(piece) for piece in pieces)


def add(parts):
    return functools.reduce(jnp.add, [part.astype(F32) for part in parts])


def swap_plane(blocks):
    return (
        blocks[0],
        lax.ppermute(blocks[1], "fsdp", ALONG_X),
        lax.ppermute(blocks[2], "fsdp", ALONG_Y),
        lax.ppermute(blocks[3], "fsdp", ACROSS),
    )


def swap_corner(block):
    half = block.shape[0] // 2
    return (lax.ppermute(block[:half], "fsdp", ALONG_X), lax.ppermute(block[half:], "fsdp", ALONG_Y))


def swap_sides(blocks, corner):
    half = blocks[1].shape[0] // 2
    to_x = jnp.concatenate([blocks[1][:half], add([blocks[1][half:], corner[1]]).astype(BF16)], axis=0)
    to_y = jnp.concatenate([add([blocks[2][:half], corner[0]]).astype(BF16), blocks[2][half:]], axis=0)
    return (blocks[0], lax.ppermute(to_x, "fsdp", ALONG_X), lax.ppermute(to_y, "fsdp", ALONG_Y))


def swap_z(blocks):
    return (blocks[0],) + tuple(to_z(blocks[k], k) for k in range(1, QUAD))


def slab(values, start, size, axis):
    return lax.dynamic_slice_in_dim(values, start, size, axis)


def tables(yx, z, core, first):
    entries = [yx ^ k for k in range(QUAD)] + [(z + k) % QUAD for k in range(QUAD)]
    entries += [core, first, 1 - core, 0, 0, 0, 0, 0]
    return jnp.stack([jnp.asarray(e, jnp.int32) for e in entries])


def gather_near(core, early, gain_attn, w_query, w_key, w_value, w_out, gain_mlp, w_gate, w_up, w_down):
    zero = core == 0
    rows = jnp.concatenate([w_out, w_query, w_key, w_value], axis=1)
    share = rows.shape[0]
    extra = ROWS - share
    pad = jnp.zeros((1, 256 - DB), BF16)
    gains = jnp.concatenate(
        [gain_attn[None], jnp.zeros((1, 256 - share), BF16), gain_mlp[None], jnp.zeros((1, FB - 256 - share), BF16)], axis=1
    )
    sent = jnp.concatenate([rows[0:extra], gains, jnp.zeros((SPARE - extra - 1, FB), BF16)], axis=0)
    taken = swap(sent)
    theirs = taken[extra : extra + 1]
    line = jnp.concatenate(
        [theirs[:, 0:share], gain_attn[None], pad, theirs[:, 256 : 256 + share], gain_mlp[None], jnp.zeros((1, FB - 256 - DB), BF16)],
        axis=1,
    )
    attn = jnp.where(
        zero,
        jnp.concatenate([rows, taken[0:extra]], axis=0),
        jnp.concatenate([jnp.broadcast_to(line, (SPARE, FB)), rows[extra:]], axis=0),
    )
    turned = w_down.T
    taken = swap(slab(turned, (1 - core) * (DB - ROWS), ROWS, 0))
    kept = slab(turned, core * (DB - ROWS), ROWS, 0)
    down = jnp.where(zero, jnp.concatenate([kept, taken], axis=1), jnp.concatenate([taken, kept], axis=1))
    taken = swap(jnp.where(zero, w_up, w_gate))
    pair = jnp.where(zero, jnp.concatenate([w_gate, taken], axis=0), jnp.concatenate([taken, w_up], axis=0))
    near_z = (from_z(pair, 1), from_z(pair, 3))
    attn = jnp.stack(spread_z(attn) + (down,))
    attn, early = lax.optimization_barrier((attn, early))
    sides = spread_sides(attn)
    other = swap(attn)
    sides, other, near_z, own = lax.optimization_barrier((sides, other, near_z, pair))
    across = spread_across(*sides)
    pair = (own, near_z[0], from_z(near_z[0], 1), near_z[1])
    across, pair, sides = lax.optimization_barrier((across, pair, sides))
    return sides + across, other, pair, early


def after(values, *others):
    return lax.optimization_barrier((values, others))[0]


def in_pieces(blocks):
    return (blocks[0], blocks[1], blocks[2], blocks[3, 0:2], blocks[3, 2:4])


def gather_any(gain_attn, w_query, w_key, w_value, w_out, gain_mlp, w_gate, w_up, w_down):
    def whole(weight):
        return lax.all_gather(lax.all_gather(weight, "dp", axis=1, tiled=True), "fsdp", axis=0, tiled=True)

    def blocks(weight):
        return weight.reshape(QUAD, weight.shape[0] // QUAD, QUAD, weight.shape[1] // QUAD).transpose(0, 2, 1, 3)

    attn = jnp.concatenate([blocks(whole(w)) for w in (w_out, w_query, w_key, w_value)], axis=3)
    gains = [lax.all_gather(g, "fsdp", axis=0, tiled=True).reshape(QUAD, 1, 1, DB) for g in (gain_attn, gain_mlp)]
    line = jnp.concatenate(
        [gains[0], jnp.zeros((QUAD, 1, 1, 256 - DB), BF16), gains[1], jnp.zeros((QUAD, 1, 1, FB - 256 - DB), BF16)], axis=3
    )
    line = jnp.broadcast_to(line, (QUAD, QUAD, SPARE, FB))
    attn_two = jnp.concatenate([line, attn[:, :, ROWS:]], axis=2)
    down = blocks(whole(w_down).T).transpose(1, 0, 2, 3)
    pair = [in_pieces(blocks(whole(w))) for w in (w_gate, w_up)]
    return (
        in_pieces(attn[:, :, 0:ROWS]) + in_pieces(attn_two),
        pair[0] + pair[1],
        tuple(down[:, z, 0:ROWS] for z in range(QUAD)) + tuple(down[:, z, DB - ROWS :] for z in range(QUAD)),
    )


def on_device(
    near,
    tokens,
    first_len,
    gain_attn,
    w_query,
    w_key,
    w_value,
    w_out,
    gain_mlp,
    w_gate,
    w_up,
    w_down,
    cotangent,
):
    length = tokens.shape[0]
    first = first_len[0]
    weights = (gain_attn, w_query, w_key, w_value, w_out, gain_mlp, w_gate, w_up, w_down)
    if near:
        place = lax.axis_index("fsdp")
        core = place & 1
        idx = tables(place >> 1, lax.axis_index("dp"), core, first)
        attn, other, pair, (idx, cosine, sine) = gather_near(core, (idx, *rope_tables(first, length)), *weights)
    else:
        core = 0
        idx = tables(0, 0, 0, first)
        attn, pair, down = gather_any(*weights)
        cosine, sine = rope_tables(first, length)
    xt, ct = tokens.T, cotangent.T
    if near:
        down = jnp.stack([attn[0][QUAD], attn[1][QUAD], attn[2][QUAD], attn[4][2]])
        attn = attn + (other,) + spread_core(attn[1:])
        pair = jnp.stack(pair)
        attn, pair, down = lax.optimization_barrier((attn, pair, down))
        pair = spread_sides(pair)
        pair_own = swap(pair[0])
        down = (down, from_z(down, 1))
    weight, gains, n1t, qx, kx, kt, vt = call_project(idx, xt, cosine, sine, attn)
    if near:
        down, pair_own, qx = lax.optimization_barrier((down, pair_own, qx))
        down = down + (from_z(down[1], 1),)
        down_core = spread_core(down[0:2])
    ot, lse = call_attend(qx, kx, vt)
    if near:
        pair, down, down_core, ot = lax.optimization_barrier((pair, down, down_core, ot))
        down = down + (from_z(down[2], 1),)
        pair = pair + spread_across(*pair)
        pair_core = (pair_own,) + spread_core(pair[1:3])
    y, n2, n2t = call_leave(xt, gains, weight, ot)
    if near:
        pair, pair_core, down, n2 = lax.optimization_barrier((pair, pair_core, down, n2))
        pair = pair + pair_core + spread_core(pair[3:5])
        down = down + down_core + spread_core(down[2:4])
    mixed, h, dgu, dyt, dat, gain_two = call_feed(idx, n2, y, ct, gains, pair, down)

    halves = gain_two[0].reshape(QUAD, 1, 2, DB // 2)
    row = jnp.pad(halves, ((0, 0), (0, 7), (0, 0), (0, FB // 2 - DB // 2))).reshape(QUAD, 8, FB)
    args_down = (ct, h, ot.reshape(D, length), dat, row)
    pair_theirs = call_pair_grads(idx, n2t, dgu)[0]
    if near:
        came = swap(pair_theirs)
        args_down = after(args_down, pair_theirs)
    else:
        came = jnp.zeros_like(pair_theirs)
    down_theirs = call_down_grads(idx, *args_down)[0]
    if near:
        came_down = swap(down_theirs)
        came = after(came, down_theirs)
    else:
        came_down = jnp.zeros_like(down_theirs)
    pair_mine = call_pair_grads(idx, n2t, dgu, received=came)
    if near:
        pair_got = swap_plane(pair_mine)
        came_down = after(came_down, pair_mine)
    down_mine = call_down_grads(idx, *args_down, received=came_down)
    if near:
        down_mine, dat = lax.optimization_barrier((down_mine, dat))
        down_corner = swap_corner(down_mine[3])
    do = call_give(weight, dat)
    heads = (qx, kx, kt, vt, ot, do, lse, cosine, sine)
    first_part = call_attend_backward(0, 2, *heads)
    if near:
        heads = after(heads, first_part)
    second_part = call_attend_backward(2, 3, *heads)
    if near:
        pair_got, down_corner, second_part = lax.optimization_barrier((pair_got, down_corner, second_part))
        pair_got = swap_z(add(pair_got).astype(BF16))
        down_got = swap_sides(down_mine, down_corner)
    parts = first_part + second_part
    grad_tokens, gain_one = call_enter_backward(idx, xt, dyt, gains, weight, *parts)
    qkv_theirs, *qkv_mine = call_qkv_grads(idx, n1t, gain_one, *parts)
    if near:
        pair_got, down_got, qkv_theirs = lax.optimization_barrier((pair_got, down_got, qkv_theirs))
        came = swap(qkv_theirs)
        qkv_got = swap_plane([add([part, came[k]]).astype(BF16) for k, part in enumerate(qkv_mine)])
        down_got = swap_z(add(down_got).astype(BF16))
        pair_sum = add(pair_got)
        qkv_got, down_got, pair_sum = lax.optimization_barrier((qkv_got, down_got, pair_sum))
        qkv_got = swap_z(add(qkv_got).astype(BF16))
        down_sum, qkv_sum = add(down_got), add(qkv_got)
        outs = settle_near(core, down_sum, pair_sum, qkv_sum)
    else:
        outs = settle_any(
            down_mine, down_theirs, pair_mine, pair_theirs, qkv_mine, qkv_theirs, gain_one[:, 0].reshape(D), gain_two[0]
        )
    return (mixed.T, grad_tokens.T) + outs


def settle_near(core, down_sum, pair_sum, qkv_sum):
    zero = core == 0
    share = DB // 2

    kept = slab(pair_sum, core * share, share, 0)
    taken = swap(slab(pair_sum, (1 - core) * share, share, 0).astype(BF16)).astype(F32)
    grad_gate, grad_up = jnp.where(zero, kept, taken), jnp.where(zero, taken, kept)

    grad_out = jnp.where(zero, down_sum[0:share, FB : FB + DB], down_sum[ROWS - share :, FB : FB + DB])
    half = FB // 2
    kept = slab(down_sum, core * half, half, 1)
    taken = swap(slab(down_sum, (1 - core) * half, half, 1).astype(BF16)).astype(F32)
    upper, lower = jnp.where(zero, kept, taken), jnp.where(zero, taken, kept)
    grad_down = jnp.concatenate([upper, lower[SPARE:]], axis=0).T
    grad_gain_mlp = lower[0, 0:share]

    kept = slab(qkv_sum, core * share, share, 1)
    taken = swap(slab(qkv_sum, (1 - core) * share, share, 1).astype(BF16)).astype(F32)
    upper, lower = jnp.where(zero, kept, taken), jnp.where(zero, taken, kept)
    grad_gain_attn = lower[0]
    rows = jnp.concatenate([upper, lower[SPARE:]], axis=0).T
    return (
        grad_gain_attn, rows[:, 0:QB], rows[:, QB : QB + KB], rows[:, QB + KB :], grad_out,
        grad_gain_mlp, grad_gate, grad_up, grad_down,
    )


def settle_any(down_mine, down_theirs, pair_mine, pair_theirs, qkv_mine, qkv_theirs, gain_one, gain_two):
    def whole(blocks):
        return blocks.transpose(0, 2, 1, 3).reshape(blocks.shape[0] * blocks.shape[2], -1)

    def shard(values):
        values = lax.psum_scatter(values, "fsdp", scatter_dimension=0, tiled=True)
        return lax.psum_scatter(values, "dp", scatter_dimension=1, tiled=True).astype(F32)

    def gain(values):
        values = lax.psum(values, "dp")
        return lax.psum_scatter(values, "fsdp", scatter_dimension=0, tiled=True)

    both = jnp.concatenate([jnp.stack(down_mine), down_theirs[:, :, SPARE:]], axis=2)
    grad_down = shard(whole(both[..., 0:FB].transpose(1, 0, 2, 3)).T)
    grad_out = shard(whole(both[..., FB : FB + DB]))
    grad_gate, grad_up = shard(whole(jnp.stack(pair_mine))), shard(whole(pair_theirs))
    both = jnp.concatenate([jnp.stack(qkv_mine), qkv_theirs[:, :, SPARE:]], axis=2).transpose(0, 1, 3, 2)
    grad_query = shard(whole(both[..., 0:QB]))
    grad_key = shard(whole(both[..., QB : QB + KB]))
    grad_value = shard(whole(both[..., QB + KB :]))
    return (
        gain(gain_one), grad_query, grad_key, grad_value, grad_out, gain(gain_two), grad_gate, grad_up, grad_down,
    )


def solution(mesh):
    sizes = dict(mesh.shape)
    near = sizes["fsdp"] == 8 and sizes["dp"] == QUAD
    in_specs = (
        P(("fsdp", "dp"), None),
        P(("fsdp", "dp")),
        P("fsdp"),
        P("fsdp", "dp"),
        P("fsdp", "dp"),
        P("fsdp", "dp"),
        P("fsdp", "dp"),
        P("fsdp"),
        P("fsdp", "dp"),
        P("fsdp", "dp"),
        P("fsdp", "dp"),
        P(("fsdp", "dp"), None),
    )
    out_specs = (
        P(("fsdp", "dp"), None),
        P(("fsdp", "dp"), None),
        P("fsdp"),
        P("fsdp", "dp"),
        P("fsdp", "dp"),
        P("fsdp", "dp"),
        P("fsdp", "dp"),
        P("fsdp"),
        P("fsdp", "dp"),
        P("fsdp", "dp"),
        P("fsdp", "dp"),
    )
    return jax.shard_map(
        functools.partial(on_device, near), mesh=mesh, in_specs=in_specs, out_specs=out_specs, check_vma=False
    )
```
